32 devices in a mesh: psg: 32 (over z, y, x, core), qry: 1.
Axes of the slice: x: 2, y: 2, z: 4, core: 2. Of those that a mesh axis runs over, the one named last changes fastest.
Arguments:
- queries: bfloat16 [1024, 4096], P('psg', 'qry'), may hold values from -6 to 6
- grad_out: bfloat16 [1024, 4096], P('psg', 'qry'), may hold values from -6 to 6
- attn_out: bfloat16 [1024, 4096], P('psg', 'qry'), may hold values from -6 to 6
- log_sum: float32 [32, 1024], P('qry', 'psg'), may hold values from 3 to 5
- keys: bfloat16 [16384, 1024], P('psg', 'qry'), may hold values from -6 to 6
- values: bfloat16 [16384, 1024], P('psg', 'qry'), may hold values from -6 to 6
- proj_weight: bfloat16 [4096, 4096], P('psg', 'qry'), may hold values from -0.09375 to 0.09375
- attend: int32 [4, 16], replicated, may hold values from 0 to 31, all different within a row; in each aligned block of 4 rows (0 to 3, 4 to 7, ...) at most 4 rows name the same one
- qlen: int32 [4], replicated, may hold values from 128 to 256, as said below
Outputs:
- grad_query: float32 [1024, 4096], P('psg', 'qry')
- grad_keys: float32 [16384, 1024], P('psg', 'qry')
- grad_values: float32 [16384, 1024], P('psg', 'qry')
- grad_hidden: float32 [1024, 4096], P('psg')
The draws below stay inside these ranges and needn't reach their ends.
Inputs may be any that keep to these rules, and one draw needn't show every extreme that they name: `attend`: each question names 16 different blocks; each block is named by at least one question and at most 4, and some block by exactly 4. `qlen`: each a multiple of 128; some question has 256 rows.
All inputs are finite; a program needn't handle non-finite values.
Results may differ from the reference program's by a relative error of at most 0.0049.
Values may be sent and summed in bfloat16 or wider, within the bound.
A program may use at most 128 MiB of HBM per device.

```python
import math
import jax
import jax.numpy as jnp
import numpy as np
from jax import lax

D = 4096
ASKING_COUNT = 32
SHARED_KV_COUNT = 8
ATTN_WIDTH = 128
GROUP = 4
PASSAGE_SPAN = 512
PASSAGES = 32
TILE = 128
QTILES = 2
PADDED_ASK_LEN = 256
NQ = 4
QROWS = 1024
TOPB = 16
CAP = 4


def draw_qlen(key, part):
    key = jax.random.fold_in(key, 11)
    first_key, second_key = jax.random.split(key)
    tiles = jax.random.randint(first_key, (NQ,), 1, QTILES + 1)
    longest = jax.random.randint(second_key, (), 0, NQ)
    tiles = jnp.where(jnp.arange(NQ) == longest, QTILES, tiles)
    return (tiles * TILE).astype(jnp.int32)


def levels(key, shape, shards, least, high):
    factor_of, own = 1.0, jax.random.fold_in(key, 6)
    for dim, blocks in shards:
        draws = jnp.exp(jax.random.uniform(jax.random.fold_in(own, dim), (blocks,), jnp.float32, least / len(shards), high / len(shards)))
        factor_of = factor_of * jnp.repeat(draws, shape[dim] // blocks).reshape([-1 if axis == dim else 1 for axis in range(len(shape))])
    return factor_of


def deal_out(stream_key, own, number, rows, amount, top, bound, lean):
    sequence = jax.random.permutation(stream_key, amount)
    packed, common = portions_of(amount, rows * top, bound, lean, True), portions_of(amount, rows * top, bound, lean, False)
    places = jnp.arange(amount)

    def named(tallies, rotation):
        used = int((tallies > 0).sum())
        fixed = max(1, used // 4)
        shifted = fixed + (places - fixed + rotation * (used - fixed)) % max(1, amount - fixed)
        return jnp.zeros((amount,), jnp.int32).at[sequence[jnp.where(places < fixed, places, shifted)]].set(jnp.asarray(tallies, jnp.int32))

    tallies = jnp.where(number % 4 == 0, named(packed, number // 4), named(common, number - number // 4 - 1))
    mixed = jax.random.permutation(jax.random.fold_in(own, 3), amount)
    donor, taker = mixed[0:amount // 2 * 2:2], mixed[1:amount // 2 * 2:2]
    room = jnp.minimum(tallies[donor] - 1, bound - tallies[taker]) // 2
    room = jnp.where((donor == sequence[0]) | (taker == sequence[0]) | (tallies[taker] == 0), 0, jnp.maximum(room, 0))
    shifted = jax.random.randint(jax.random.fold_in(own, 4), (amount // 2,), 0, 1 << 20) % (room + 1)
    tallies = tallies.at[donor].add(-shifted).at[taker].add(shifted)
    items = jnp.searchsorted(jnp.cumsum(tallies), jnp.arange(rows * top), side="right").astype(jnp.int32)
    listing = items.reshape(top, rows).T
    listing = listing[jax.random.permutation(jax.random.fold_in(own, 1), rows)]
    rotation = jax.random.randint(jax.random.fold_in(own, 2), (rows, 1), 0, top)
    return jnp.take_along_axis(listing, (jnp.arange(top)[None, :] + rotation) % top, axis=1)


def portions_of(amount, total, most, skew, full):
    loads = [(1 << 20) // math.isqrt(grade ** skew) + 1 for grade in range(1, amount + 1)]
    largest = most if full else min(most, max(-(-total // amount), total * loads[0] // sum(loads)))
    least = 1 if total - largest >= amount - 1 else 0
    given, surplus = [largest] + [least] * (amount - 1), total - largest - least * (amount - 1)
    while surplus > 0:
        candidates = [i for i in range(1, amount) if given[i] < largest] or [i for i in range(1, amount) if given[i] < most]
        whole, remaining = sum([loads[i] for i in candidates]), surplus
        for i in candidates:
            addition = min(most - given[i], max(1, remaining * loads[i] // whole), surplus)
            given[i] = given[i] + addition
            surplus = surplus - addition
    return np.array(given)


def bell_draw(rng, dims, width, reach, pieces=(), kind=jnp.bfloat16):
    level = levels(rng, dims, pieces, -0.22, 0.18) if pieces else 1.0
    values = jax.random.normal(rng, dims, jnp.float32) * width * level
    return jnp.minimum(jnp.maximum(values, -reach), reach).astype(kind)


def setup_inputs(seed: int = 0) -> dict:
    key_list = jax.random.split(jax.random.key(seed), 10)
    queries = bell_draw(key_list[0], (QROWS, ASKING_COUNT * ATTN_WIDTH), 1.0, 6.0, ((0, 32),))
    grad_out = bell_draw(key_list[1], (QROWS, ASKING_COUNT * ATTN_WIDTH), 1.0, 6.0, ((0, 32),))
    attn_out = bell_draw(key_list[2], (QROWS, ASKING_COUNT * ATTN_WIDTH), 1.0, 6.0, ((0, 32),))
    log_sum = jnp.clip(3.0 + 2.0 * jax.random.uniform(key_list[3], (ASKING_COUNT, QROWS), jnp.float32) ** levels(key_list[3], (ASKING_COUNT, QROWS), ((1, 32),), -0.2, 0.2), 3.0, 5.0)
    keys = bell_draw(key_list[4], (PASSAGES * PASSAGE_SPAN, SHARED_KV_COUNT * ATTN_WIDTH), 1.0, 6.0, ((0, 32),))
    values = bell_draw(key_list[5], (PASSAGES * PASSAGE_SPAN, SHARED_KV_COUNT * ATTN_WIDTH), 1.0, 6.0, ((0, 32),))
    proj_weight = bell_draw(key_list[6], (D, ASKING_COUNT * ATTN_WIDTH), (ASKING_COUNT * ATTN_WIDTH) ** -0.5, 0.09375, ((0, 32),))
    attend_keys = jax.random.split(jax.random.fold_in(key_list[7], 1), NQ // NQ)
    attend_turns = jax.random.permutation(jax.random.fold_in(key_list[7], 3), NQ // NQ)
    attend = jax.vmap(lambda own, number: deal_out(jax.random.fold_in(key_list[7], 2), own, number, NQ, PASSAGES, TOPB, CAP, 2))(attend_keys, attend_turns).reshape((NQ, TOPB))
    qlen = draw_qlen(jax.random.fold_in(key_list[9], 71), 0)
    return {"queries": queries, "grad_out": grad_out, "attn_out": attn_out, "log_sum": log_sum, "keys": keys, "values": values, "proj_weight": proj_weight, "attend": attend, "qlen": qlen}


def row_delta(grad_out, attn_out):
    products = grad_out.astype(jnp.float32) * attn_out.astype(jnp.float32)
    return jnp.sum(products.reshape(products.shape[0], ASKING_COUNT, ATTN_WIDTH), axis=2).T


def reference(queries, grad_out, attn_out, log_sum, keys, values, proj_weight, attend, qlen):
    inverse_root_dimension = ATTN_WIDTH ** -0.5
    delta = row_delta(grad_out, attn_out)

    def visit(totals, pair_index):
        grad_q, grad_k, grad_v = totals
        question = pair_index // TOPB
        passage = attend[question, pair_index % TOPB]
        row_start = (question * PADDED_ASK_LEN).astype(jnp.int32)
        key_start = (passage * PASSAGE_SPAN).astype(jnp.int32)
        asking_matrix_tile = lax.dynamic_slice_in_dim(queries, row_start, PADDED_ASK_LEN, 0).astype(jnp.float32).reshape(PADDED_ASK_LEN, SHARED_KV_COUNT, GROUP, ATTN_WIDTH)
        output_gradient_rows = lax.dynamic_slice_in_dim(grad_out, row_start, PADDED_ASK_LEN, 0).astype(jnp.float32).reshape(PADDED_ASK_LEN, SHARED_KV_COUNT, GROUP, ATTN_WIDTH)
        passage_lookup_matrix = lax.dynamic_slice_in_dim(keys, key_start, PASSAGE_SPAN, 0).astype(jnp.float32).reshape(PASSAGE_SPAN, SHARED_KV_COUNT, ATTN_WIDTH)
        value_block_rows = lax.dynamic_slice_in_dim(values, key_start, PASSAGE_SPAN, 0).astype(jnp.float32).reshape(PASSAGE_SPAN, SHARED_KV_COUNT, ATTN_WIDTH)
        lse_rows = lax.dynamic_slice_in_dim(log_sum, row_start, PADDED_ASK_LEN, 1).reshape(SHARED_KV_COUNT, GROUP, PADDED_ASK_LEN)
        delta_rows = lax.dynamic_slice_in_dim(delta, row_start, PADDED_ASK_LEN, 1).reshape(SHARED_KV_COUNT, GROUP, PADDED_ASK_LEN)
        row_valid = (jnp.arange(PADDED_ASK_LEN) < qlen[question]).astype(jnp.float32)
        raw_attention_energies = jnp.einsum('dlyb,ilb->lydi', asking_matrix_tile, passage_lookup_matrix) * inverse_root_dimension
        probs = jnp.exp(raw_attention_energies - lse_rows[..., None]) * row_valid[None, None, :, None]
        probability_narrow = lax.optimization_barrier(probs.astype(jnp.bfloat16)).astype(jnp.float32)
        probability_gradient = jnp.einsum('dlyb,ilb->lydi', output_gradient_rows, value_block_rows)
        dscore = probs * (probability_gradient - delta_rows[..., None])
        energy_derivative_lowprec = lax.optimization_barrier(dscore.astype(jnp.bfloat16)).astype(jnp.float32)
        asking_partial_term = (jnp.einsum('ilgy,yiu->gilu', energy_derivative_lowprec, passage_lookup_matrix) * inverse_root_dimension).reshape(PADDED_ASK_LEN, ASKING_COUNT * ATTN_WIDTH)
        lookup_partial_term = (jnp.einsum('nwde,dnwj->enj', energy_derivative_lowprec, asking_matrix_tile) * inverse_root_dimension).reshape(PASSAGE_SPAN, SHARED_KV_COUNT * ATTN_WIDTH)
        value_contribution = jnp.einsum('nwde,dnwj->enj', probability_narrow, output_gradient_rows).reshape(PASSAGE_SPAN, SHARED_KV_COUNT * ATTN_WIDTH)
        grad_q = lax.dynamic_update_slice_in_dim(grad_q, lax.dynamic_slice_in_dim(grad_q, row_start, PADDED_ASK_LEN, 0) + asking_partial_term, row_start, 0)
        grad_k = lax.dynamic_update_slice_in_dim(grad_k, lax.dynamic_slice_in_dim(grad_k, key_start, PASSAGE_SPAN, 0) + lookup_partial_term, key_start, 0)
        grad_v = lax.dynamic_update_slice_in_dim(grad_v, lax.dynamic_slice_in_dim(grad_v, key_start, PASSAGE_SPAN, 0) + value_contribution, key_start, 0)
        return (grad_q, grad_k, grad_v), None

    start_totals = (jnp.zeros((QROWS, ASKING_COUNT * ATTN_WIDTH), jnp.float32),
                    jnp.zeros((PASSAGES * PASSAGE_SPAN, SHARED_KV_COUNT * ATTN_WIDTH), jnp.float32),
                    jnp.zeros((PASSAGES * PASSAGE_SPAN, SHARED_KV_COUNT * ATTN_WIDTH), jnp.float32))
    totals, unused = lax.scan(visit, start_totals, jnp.arange(NQ * TOPB, dtype=jnp.int32))
    grad_query, grad_keys, grad_values = totals
    grad_hidden = jnp.dot(grad_query.astype(jnp.bfloat16), proj_weight.T, preferred_element_type=jnp.float32)
    return grad_query, grad_keys, grad_values, grad_hidden
```

```python
import functools

import jax
import jax.numpy as jnp
from jax import lax
from jax.experimental import pallas as pl
from jax.experimental.pallas import tpu as pltpu
from jax.sharding import PartitionSpec as P

ATTN_WIDTH = 128
GROUP = 4
PADDED_ASK_LEN = 256
TILE = 128
LOG2_E = 1.4426950408889634
SCALE = ATTN_WIDTH ** (-0.5)
NT = (((1,), (1,)), ((), ()))
NN = (((1,), (0,)), ((), ()))


def dot(a, b, dims=NN):
    return lax.dot_general(a, b, dims, preferred_element_type=jnp.float32)


def attention_kernel(
    blocks, tile_count, counts, tiles, kv_ref, q_ref, g_ref, ld_ref, dkv_ref, dq_ref, dk_acc, dv_acc, dq_acc
):
    block = pl.program_id(0)

    @pl.when(block == 0)
    def _():
        dq_acc[...] = jnp.zeros_like(dq_acc)

    dk_acc[...] = jnp.zeros_like(dk_acc)
    dv_acc[...] = jnp.zeros_like(dv_acc)
    key_rows_t = kv_ref[0, 0].T

    def visit(i, carry):
        tile = tiles[block, i]
        keys, values = kv_ref[0, 0], kv_ref[0, 1]
        dk, dv = None, None
        for part in range(2):
            rows = slice(part * 256, part * 256 + 256)
            q = q_ref[tile, rows, :]
            g = g_ref[tile, rows, :]
            lse = ld_ref[tile, 0:1, rows]
            delta = ld_ref[tile, 1:2, rows]
            prob = jnp.exp2(dot(keys, q, NT) * (SCALE * LOG2_E) - lse)
            dprob = dot(values, g, NT)
            dscore = (prob * (dprob - delta)).astype(jnp.bfloat16)
            v_term = dot(prob.astype(jnp.bfloat16), g)
            k_term = dot(dscore, q)
            dv = v_term if dv is None else dv + v_term
            dk = k_term if dk is None else dk + k_term
            dq_acc[tile, :, rows] += dot(key_rows_t, dscore)
        dk_acc[...] += dk
        dv_acc[...] += dv
        return carry

    lax.fori_loop(0, counts[block], visit, 0)
    dkv_ref[0, 0] = (dk_acc[...] * SCALE).astype(dkv_ref.dtype)
    dkv_ref[0, 1] = dv_acc[...].astype(dkv_ref.dtype)

    @pl.when(block == blocks - 1)
    def _():
        def put(tile, carry):
            for h in range(GROUP):
                cols = slice(h * ATTN_WIDTH, (h + 1) * ATTN_WIDTH)
                piece = dq_acc[tile, :, cols] * SCALE
                dq_ref[tile, :, cols] = piece.T.astype(dq_ref.dtype)
            return carry

        lax.fori_loop(0, tile_count, put, 0)


def attention(counts, tiles, kv, q, g, ld, out_dtype):
    blocks, _, span, width = kv.shape
    tile_count, lanes, _ = q.shape
    whole = lambda shape: pl.BlockSpec(shape, lambda b, *_: (0,) * len(shape))
    return pl.pallas_call(
        functools.partial(attention_kernel, blocks, tile_count),
        out_shape=(
            jax.ShapeDtypeStruct(kv.shape, out_dtype),
            jax.ShapeDtypeStruct((tile_count, TILE, lanes), jnp.bfloat16),
        ),
        grid_spec=pltpu.PrefetchScalarGridSpec(
            num_scalar_prefetch=2,
            grid=(blocks,),
            in_specs=[
                pl.BlockSpec((1, 2, span, width), lambda b, *_: (b, 0, 0, 0)),
                whole(q.shape),
                whole(g.shape),
                whole(ld.shape),
            ],
            out_specs=(
                pl.BlockSpec((1, 2, span, width), lambda b, *_: (b, 0, 0, 0)),
                whole((tile_count, TILE, lanes)),
            ),
            scratch_shapes=[
                pltpu.VMEM((span, width), jnp.float32),
                pltpu.VMEM((span, width), jnp.float32),
                pltpu.VMEM((tile_count, width, lanes), jnp.float32),
            ],
        ),
        compiler_params=pltpu.CompilerParams(vmem_limit_bytes=48 * 2**20),
        cost_estimate=pl.CostEstimate(
            flops=2 * blocks * span * width * lanes * tile_count * 5 // 2,
            bytes_accessed=16 * 2**20,
            transcendentals=blocks * span * lanes * tile_count // 2,
        ),
        name="attention",
    )(counts, tiles, kv, q, g, ld)


def on_device(queries, grad_out, attn_out, log_sum, keys, values, proj_weight, attend, qlen):
    row_count, columns = queries.shape
    head_count = log_sum.shape[0]
    slices = head_count // GROUP
    span = keys.shape[0]
    devices = lax.axis_size("psg")
    layers = devices // slices
    me = lax.axis_index("psg")
    lanes = GROUP * ATTN_WIDTH
    peers = [[z * slices + j for j in range(slices)] for z in range(layers)]
    per_tile = TILE // row_count
    tile_count = devices // per_tile

    kv = jnp.stack([keys, values]).reshape(2, span, slices, ATTN_WIDTH).transpose(2, 0, 1, 3)
    if slices > 1:
        kv = lax.all_to_all(kv, "psg", 0, 0, axis_index_groups=peers)

    qg = jnp.stack([queries, grad_out]).reshape(2, row_count, slices, GROUP, ATTN_WIDTH)
    qg = qg.transpose(2, 0, 3, 1, 4)
    qg = jnp.broadcast_to(qg[None], (layers,) + qg.shape).reshape((devices,) + qg.shape[1:])
    qg = lax.all_to_all(qg, "psg", 0, 0)
    qg = qg.reshape(tile_count, per_tile, 2, GROUP, row_count, ATTN_WIDTH)
    qg = qg.transpose(2, 0, 3, 1, 4, 5).reshape(2, tile_count, lanes, ATTN_WIDTH)

    products = grad_out.astype(jnp.float32) * attn_out.astype(jnp.float32)
    delta = jnp.sum(products.reshape(row_count, head_count, ATTN_WIDTH), axis=2).T
    ld = jnp.stack([log_sum * LOG2_E, delta])
    ld = ld.reshape(2, slices, GROUP, row_count).transpose(1, 0, 2, 3)
    ld = jnp.broadcast_to(ld[None], (layers,) + ld.shape).reshape((devices,) + ld.shape[1:])
    ld = lax.all_to_all(ld, "psg", 0, 0)
    ld = ld.reshape(tile_count, per_tile, 2, GROUP, row_count)
    ld = ld.transpose(0, 2, 3, 1, 4).reshape(tile_count, 2, lanes)

    block_ids = (me // slices) * slices + jnp.arange(slices, dtype=jnp.int32)
    named = jnp.any(attend[None] == block_ids[:, None, None], axis=2)
    tile_ids = jnp.arange(tile_count, dtype=jnp.int32)
    tile_start = tile_ids * TILE % PADDED_ASK_LEN
    tile_live = tile_start < jnp.repeat(qlen, PADDED_ASK_LEN // TILE)
    live = jnp.repeat(named, PADDED_ASK_LEN // TILE, axis=1) & tile_live[None]
    rank = jnp.cumsum(live.astype(jnp.int32), axis=1) - 1
    chosen = live[:, None, :] & (rank[:, None, :] == tile_ids[None, :, None])
    tiles = jnp.sum(jnp.where(chosen, tile_ids[None, None, :], 0), axis=2).astype(jnp.int32)
    counts = jnp.sum(live.astype(jnp.int32), axis=1)

    out_dtype = jnp.bfloat16 if slices > 1 else jnp.float32
    dkv, dq = attention(counts, tiles, kv, qg[0], qg[1], ld, out_dtype)

    dq = lax.all_to_all(dq.reshape(devices, row_count, lanes), "psg", 0, 0)
    dq = dq.reshape(layers, slices, row_count, lanes).astype(jnp.float32)
    grad_query = jnp.sum(dq, axis=0).transpose(1, 0, 2).reshape(row_count, columns)
    query_low = grad_query.astype(jnp.bfloat16)

    all_low = lax.all_gather(query_low, "psg", axis=0, tiled=True)
    hidden = dot(all_low, proj_weight, NT)
    out_columns = proj_weight.shape[0]
    hidden = lax.all_to_all(hidden.reshape(devices, row_count, out_columns), "psg", 0, 0)
    hidden = hidden.transpose(1, 0, 2).reshape(row_count, devices * out_columns)
    grad_hidden = lax.psum(hidden, "qry")

    if slices > 1:
        dkv = lax.all_to_all(dkv, "psg", 0, 0, axis_index_groups=peers)
    dkv = dkv.astype(jnp.float32).transpose(1, 2, 0, 3).reshape(2, span, slices * ATTN_WIDTH)
    return (grad_query, dkv[0], dkv[1], grad_hidden)


def solution(mesh):
    in_specs = (
        P("psg", "qry"),
        P("psg", "qry"),
        P("psg", "qry"),
        P("qry", "psg"),
        P("psg", "qry"),
        P("psg", "qry"),
        P("psg", "qry"),
        P(),
        P(),
    )
    out_specs = (P("psg", "qry"), P("psg", "qry"), P("psg", "qry"), P("psg", None))
    return jax.shard_map(
        on_device, mesh=mesh, in_specs=in_specs, out_specs=out_specs, check_vma=False
    )
```

```python
import functools

import jax
import jax.numpy as jnp
from jax import lax
from jax.experimental import pallas as pl
from jax.experimental.pallas import tpu as pltpu
from jax.sharding import PartitionSpec as P

ATTN_WIDTH = 128
GROUP = 4
PADDED_ASK_LEN = 256
TILE = 128
LOG2_E = 1.4426950408889634
SCALE = ATTN_WIDTH ** (-0.5)
NT = (((1,), (1,)), ((), ()))
NN = (((1,), (0,)), ((), ()))


def dot(a, b, dims=NN):
    return lax.dot_general(a, b, dims, preferred_element_type=jnp.float32)


def attention_kernel(
    blocks, tile_count, per_tile, counts, tiles, kv_ref, qg_ref, ld_ref, dkv_ref, dq_ref, dk_acc, dv_acc, dq_acc
):
    block = pl.program_id(0)
    per_part = per_tile // 2
    wide = GROUP * TILE // per_tile

    @pl.when(block == 0)
    def _():
        dq_acc[...] = jnp.zeros_like(dq_acc)

    dk_acc[...] = jnp.zeros_like(dk_acc)
    dv_acc[...] = jnp.zeros_like(dv_acc)
    key_rows_t = kv_ref[0, 0].T

    def visit(i, carry):
        tile = tiles[block, i]
        keys, values = kv_ref[0, 0], kv_ref[0, 1]
        dk, dv = None, None
        for part in range(2):
            rows = slice(part * 256, part * 256 + 256)
            first = tile * per_tile + part * per_part
            q = qg_ref[pl.ds(first, per_part), 0].reshape(256, ATTN_WIDTH)
            g = qg_ref[pl.ds(first, per_part), 1].reshape(256, ATTN_WIDTH)
            ld = jnp.concatenate([ld_ref[first + k] for k in range(per_part)], axis=1)
            lse, delta = ld[0:1], ld[1:2]
            prob = jnp.exp2(dot(keys, q, NT) * (SCALE * LOG2_E) - lse)
            dprob = dot(values, g, NT)
            dscore = (prob * (dprob - delta)).astype(jnp.bfloat16)
            v_term = dot(prob.astype(jnp.bfloat16), g)
            k_term = dot(dscore, q)
            dv = v_term if dv is None else dv + v_term
            dk = k_term if dk is None else dk + k_term
            dq_acc[tile, :, rows] += dot(key_rows_t, dscore)
        dk_acc[...] += dk
        dv_acc[...] += dv
        return carry

    lax.fori_loop(0, counts[block], visit, 0)
    dkv_ref[0, 0] = (dk_acc[...] * SCALE).astype(dkv_ref.dtype)
    dkv_ref[0, 1] = dv_acc[...].astype(dkv_ref.dtype)

    @pl.when(block == blocks - 1)
    def _():
        def put(tile, carry):
            for k in range(per_tile):
                piece = dq_acc[tile, :, k * wide : (k + 1) * wide] * SCALE
                dq_ref[tile * per_tile + k] = piece.T.astype(dq_ref.dtype)
            return carry

        lax.fori_loop(0, tile_count, put, 0)


def attention(counts, tiles, kv, qg, ld, out_dtype):
    blocks, _, span, width = kv.shape
    sources, _, wide, _ = qg.shape
    lanes = GROUP * TILE
    per_tile = lanes // wide
    tile_count = sources // per_tile
    whole = lambda shape: pl.BlockSpec(shape, lambda b, *_: (0,) * len(shape))
    return pl.pallas_call(
        functools.partial(attention_kernel, blocks, tile_count, per_tile),
        out_shape=(
            jax.ShapeDtypeStruct(kv.shape, out_dtype),
            jax.ShapeDtypeStruct((sources, wide, width), jnp.bfloat16),
        ),
        grid_spec=pltpu.PrefetchScalarGridSpec(
            num_scalar_prefetch=2,
            grid=(blocks,),
            in_specs=[
                pl.BlockSpec((1, 2, span, width), lambda b, *_: (b, 0, 0, 0)),
                whole(qg.shape),
                whole(ld.shape),
            ],
            out_specs=(
                pl.BlockSpec((1, 2, span, width), lambda b, *_: (b, 0, 0, 0)),
                whole((sources, wide, width)),
            ),
            scratch_shapes=[
                pltpu.VMEM((span, width), jnp.float32),
                pltpu.VMEM((span, width), jnp.float32),
                pltpu.VMEM((tile_count, width, lanes), jnp.float32),
            ],
        ),
        compiler_params=pltpu.CompilerParams(vmem_limit_bytes=48 * 2**20),
        cost_estimate=pl.CostEstimate(
            flops=2 * blocks * span * width * lanes * tile_count * 5 // 2,
            bytes_accessed=16 * 2**20,
            transcendentals=blocks * span * lanes * tile_count // 2,
        ),
        name="attention",
    )(counts, tiles, kv, qg, ld)


def routes(kind, devices, slices, me):
    layers = devices // slices
    j, z = lax.rem(me, slices), me // slices
    base = me - j
    if kind in ("all", "cast"):

        def step(r):
            target = lax.rem(me + r, devices)
            return target, (target if kind == "all" else lax.rem(target, slices)), me

        return devices, step
    if kind == "layer":

        def step(r):
            other = lax.rem(j + r, slices)
            return base + other, other, j

        return slices, step
    if kind == "z":

        def step(r):
            other = lax.rem(z + r, layers)
            return other * slices + j, other, z

        return layers, step
    quads = slices // 2

    def step(r):
        other = lax.rem(j // 2 + r, quads)
        return base + 2 * other + lax.rem(j, 2), other, j // 2

    return quads, step


def repeat(first, count, body):
    if count - first <= 8:
        for r in range(first, count):
            body(r)
    else:
        lax.fori_loop(first, count, lambda r, c: (body(r), c)[1], 0)


def exchange_kernel(kinds, devices, slices, gathered, *refs):
    n = len(kinds)
    total = n + gathered
    sources, outs = refs[:total], refs[total : 2 * total]
    sems = refs[2 * total :]
    me = lax.axis_index("psg")
    barrier = pltpu.get_barrier_semaphore()
    if "all" in kinds or "cast" in kinds:
        greeted = ("all",)
    else:
        greeted = ("z", "layer")
    count = 0
    for kind in greeted:
        size, step = routes(kind, devices, slices, me)
        count += size - 1

        def greet(r, step=step):
            pl.semaphore_signal(barrier, inc=1, device_id={"psg": step(r)[0]}, device_id_type=pl.DeviceIdType.MESH)

        repeat(1, size, greet)
    pl.semaphore_wait(barrier, count)

    def remote(src, dst, send, recv, target):
        return pltpu.make_async_remote_copy(
            src_ref=src,
            dst_ref=dst,
            send_sem=send,
            recv_sem=recv,
            device_id={"psg": target},
            device_id_type=pl.DeviceIdType.MESH,
        )

    if gathered:
        j, z = lax.rem(me, slices), me // slices
        parity = lax.rem(j, 2)
        partner = me + 1 - 2 * parity
        layers = devices // slices
        mine, pair = sources[n], outs[n]
        send, recv, pair_send, pair_recv, own = sems[3 * n :]
        along = []
        for r in range(1, layers):
            target = lax.rem(z + r, layers) * slices + j
            along.append(remote(mine, pair.at[parity, z], send.at[r], recv.at[r], target))
            along[-1].start()
        across = [remote(mine, pair.at[parity, z], pair_send.at[0], pair_recv.at[0], partner)]
        across[0].start()
        kept = pltpu.make_async_copy(mine, pair.at[parity, z], own)
        kept.start()

    moves, stays = [], []
    for i, kind in enumerate(kinds):
        size, step = routes(kind, devices, slices, me)

        def copy(r, i=i, step=step):
            target, chunk, slot = step(r)
            return remote(
                sources[i].at[chunk], outs[i].at[slot], sems[3 * i].at[r], sems[3 * i + 1].at[r], target
            )

        moves.append((size, copy))
        chunk, slot = step(0)[1:]
        stays.append(pltpu.make_async_copy(sources[i].at[chunk], outs[i].at[slot], sems[3 * i + 2]))
    for size, copy in moves:
        repeat(1, size, lambda r, copy=copy: copy(r).start())
    for stay in stays:
        stay.start()

    if gathered:
        for r in range(1, layers):
            along[r - 1].wait_recv()
            landed = pair.at[parity, lax.rem(z - r + layers, layers)]
            across.append(remote(landed, landed, pair_send.at[r], pair_recv.at[r], partner))
            across[-1].start()
        for copy in along:
            copy.wait_send()
        for copy in across:
            copy.wait()
        kept.wait()
    for stay in stays:
        stay.wait()
    for size, copy in moves:
        repeat(1, size, lambda r, copy=copy: copy(r).wait())


def exchange(name, number, devices, slices, parts, gather=None):
    kinds = tuple(kind for kind, _ in parts)
    arrays = [array for _, array in parts]
    layers = devices // slices
    sizes = {"all": devices, "cast": devices, "layer": slices, "z": layers, "parity": slices // 2}
    shapes = [
        jax.ShapeDtypeStruct((sizes[kind],) + array.shape[1:], array.dtype) for kind, array in parts
    ]
    scratch = []
    for kind in kinds:
        scratch += [pltpu.SemaphoreType.DMA((sizes[kind],))] * 2 + [pltpu.SemaphoreType.DMA]
    if gather is not None:
        arrays.append(gather)
        shapes.append(jax.ShapeDtypeStruct((2, layers) + gather.shape, gather.dtype))
        scratch += [pltpu.SemaphoreType.DMA((layers,))] * 4 + [pltpu.SemaphoreType.DMA]
    anywhere = pl.BlockSpec(memory_space=pl.ANY)
    return pl.pallas_call(
        functools.partial(exchange_kernel, kinds, devices, slices, int(gather is not None)),
        out_shape=tuple(shapes),
        in_specs=[anywhere] * len(arrays),
        out_specs=tuple([anywhere] * len(shapes)),
        scratch_shapes=scratch,
        compiler_params=pltpu.CompilerParams(collective_id=number, has_side_effects=True),
        cost_estimate=pl.CostEstimate(flops=0, bytes_accessed=60 * 2**20, transcendentals=0),
        name=name,
    )(*arrays)


def on_device(queries, grad_out, attn_out, log_sum, keys, values, proj_weight, attend, qlen):
    row_count, columns = queries.shape
    head_count = log_sum.shape[0]
    slices = head_count // GROUP
    span = keys.shape[0]
    devices = lax.axis_size("psg")
    layers = devices // slices
    me = lax.axis_index("psg")
    lanes = GROUP * ATTN_WIDTH
    wide = GROUP * row_count
    tile_count = devices * row_count // TILE
    run = functools.partial(exchange, devices=devices, slices=slices)

    kv = jnp.stack([keys, values]).reshape(2, span, slices, ATTN_WIDTH).transpose(2, 0, 1, 3)
    qg = jnp.stack([queries, grad_out]).reshape(2, row_count, slices, GROUP, ATTN_WIDTH)
    qg = qg.transpose(2, 0, 3, 1, 4).reshape(slices, 2, wide, ATTN_WIDTH)
    products = grad_out.astype(jnp.float32) * attn_out.astype(jnp.float32)
    delta = jnp.sum(products.reshape(row_count, head_count, ATTN_WIDTH), axis=2).T
    ld = jnp.stack([log_sum * LOG2_E, delta])
    ld = ld.reshape(2, slices, wide).transpose(1, 0, 2)
    if slices > 1:
        qg, ld, kv = run("exchange_in", 0, parts=[("cast", qg), ("cast", ld), ("layer", kv)])
    else:
        qg, ld = run("exchange_in", 0, parts=[("cast", qg), ("cast", ld)])

    block_ids = (me // slices) * slices + jnp.arange(slices, dtype=jnp.int32)
    named = jnp.any(attend[None] == block_ids[:, None, None], axis=2)
    tile_ids = jnp.arange(tile_count, dtype=jnp.int32)
    tile_start = tile_ids * TILE % PADDED_ASK_LEN
    tile_live = tile_start < jnp.repeat(qlen, PADDED_ASK_LEN // TILE)
    live = jnp.repeat(named, PADDED_ASK_LEN // TILE, axis=1) & tile_live[None]
    rank = jnp.cumsum(live.astype(jnp.int32), axis=1) - 1
    chosen = live[:, None, :] & (rank[:, None, :] == tile_ids[None, :, None])
    tiles = jnp.sum(jnp.where(chosen, tile_ids[None, None, :], 0), axis=2).astype(jnp.int32)
    counts = jnp.sum(live.astype(jnp.int32), axis=1)

    out_dtype = jnp.bfloat16 if slices > 1 else jnp.float32
    dkv, dq = attention(counts, tiles, kv, qg, ld, out_dtype)

    dq = dq.reshape(layers, slices, wide, ATTN_WIDTH)
    if slices > 1:
        dq, dkv = run("exchange_terms", 1, parts=[("z", dq), ("layer", dkv)])
    else:
        (dq,) = run("exchange_terms", 1, parts=[("all", dq)])
    summed = jnp.sum(dq.astype(jnp.float32), axis=0)
    low = summed.astype(jnp.bfloat16).reshape(slices, GROUP, row_count, ATTN_WIDTH)
    low = low.transpose(0, 2, 1, 3).reshape(slices * row_count, lanes)

    out_columns = proj_weight.shape[0]
    if slices > 1:
        weight = proj_weight.reshape(out_columns, slices // 2, 2 * lanes).transpose(1, 0, 2)
        summed, weight, low = run(
            "exchange_rows", 2, parts=[("layer", summed), ("parity", weight)], gather=low
        )
        low = low.reshape(2, devices * row_count, lanes)
        weight = weight.reshape(slices // 2 * out_columns, 2 * lanes)
        hidden = dot(low[0], weight[:, :lanes], NT) + dot(low[1], weight[:, lanes:], NT)
        hidden = hidden.astype(jnp.bfloat16).reshape(devices, row_count, slices // 2 * out_columns)
        (hidden,) = run("exchange_hidden", 3, parts=[("all", hidden)])
        hidden = hidden.reshape(layers, slices // 2, 2, row_count, slices // 2, out_columns)
        hidden = jnp.sum(hidden.astype(jnp.float32), axis=1)
        hidden = hidden.transpose(2, 0, 3, 1, 4).reshape(row_count, devices * out_columns)
    else:
        all_low = lax.all_gather(low, "psg", axis=0, tiled=True)
        hidden = dot(all_low, proj_weight, NT)
        hidden = lax.all_to_all(hidden.reshape(devices, row_count, out_columns), "psg", 0, 0)
        hidden = hidden.transpose(1, 0, 2).reshape(row_count, devices * out_columns)
    grad_hidden = lax.psum(hidden, "qry")

    grad_query = summed.reshape(slices, GROUP, row_count, ATTN_WIDTH)
    grad_query = grad_query.transpose(2, 0, 1, 3).reshape(row_count, columns)
    dkv = dkv.astype(jnp.float32).transpose(1, 2, 0, 3).reshape(2, span, slices * ATTN_WIDTH)
    return (grad_query, dkv[0], dkv[1], grad_hidden)


def solution(mesh):
    in_specs = (
        P("psg", "qry"),
        P("psg", "qry"),
        P("psg", "qry"),
        P("qry", "psg"),
        P("psg", "qry"),
        P("psg", "qry"),
        P("psg", "qry"),
        P(),
        P(),
    )
    out_specs = (P("psg", "qry"), P("psg", "qry"), P("psg", "qry"), P("psg", None))
    return jax.shard_map(
        on_device, mesh=mesh, in_specs=in_specs, out_specs=out_specs, check_vma=False
    )
```

```python
import functools

import jax
import jax.numpy as jnp
from jax import lax
from jax.experimental import pallas as pl
from jax.experimental.pallas import tpu as pltpu
from jax.sharding import PartitionSpec as P

ATTN_WIDTH = 128
GROUP = 4
PADDED_ASK_LEN = 256
TILE = 128
LOG2_E = 1.4426950408889634
SCALE = ATTN_WIDTH ** (-0.5)
NT = (((1,), (1,)), ((), ()))
NN = (((1,), (0,)), ((), ()))


def dot(a, b, dims=NN):
    return lax.dot_general(a, b, dims, preferred_element_type=jnp.float32)


def head_rows(qg_ref, first, per_part, which):
    pieces = [
        qg_ref[first + k, which, :, h * ATTN_WIDTH : (h + 1) * ATTN_WIDTH]
        for k in range(per_part)
        for h in range(GROUP)
    ]
    return jnp.concatenate(pieces, axis=0)


def attention_kernel(
    blocks, tile_count, per_tile, counts, tiles, kv_ref, qg_ref, ld_ref, dkv_ref, dq_ref, dk_acc, dv_acc, dq_acc
):
    block = pl.program_id(0)
    per_part = per_tile // 2
    row_count = TILE // per_tile
    wide = GROUP * row_count

    @pl.when(block == 0)
    def _():
        dq_acc[...] = jnp.zeros_like(dq_acc)

    dk_acc[...] = jnp.zeros_like(dk_acc)
    dv_acc[...] = jnp.zeros_like(dv_acc)
    key_rows_t = kv_ref[0, 0].T

    def visit(i, carry):
        tile = tiles[block, i]
        keys, values = kv_ref[0, 0], kv_ref[0, 1]
        dk, dv = None, None
        for part in range(2):
            rows = slice(part * 256, part * 256 + 256)
            first = tile * per_tile + part * per_part
            q = head_rows(qg_ref, first, per_part, 0)
            g = head_rows(qg_ref, first, per_part, 1)
            ld = jnp.concatenate([ld_ref[first + k] for k in range(per_part)], axis=1)
            lse, delta = ld[0:1], ld[1:2]
            prob = jnp.exp2(dot(keys, q, NT) * (SCALE * LOG2_E) - lse)
            dprob = dot(values, g, NT)
            dscore = (prob * (dprob - delta)).astype(jnp.bfloat16)
            v_term = dot(prob.astype(jnp.bfloat16), g)
            k_term = dot(dscore, q)
            dv = v_term if dv is None else dv + v_term
            dk = k_term if dk is None else dk + k_term
            dq_acc[tile, :, rows] += dot(key_rows_t, dscore)
        dk_acc[...] += dk
        dv_acc[...] += dv
        return carry

    lax.fori_loop(0, counts[block], visit, 0)
    dkv_ref[0, 0] = (dk_acc[...] * SCALE).astype(dkv_ref.dtype)
    dkv_ref[0, 1] = dv_acc[...].astype(dkv_ref.dtype)

    @pl.when(block == blocks - 1)
    def _():
        def put(tile, carry):
            for k in range(per_tile):
                piece = dq_acc[tile, :, k * wide : (k + 1) * wide] * SCALE
                piece = piece.T.astype(dq_ref.dtype)
                for h in range(GROUP):
                    cols = slice(h * ATTN_WIDTH, (h + 1) * ATTN_WIDTH)
                    dq_ref[tile * per_tile + k, :, cols] = piece[h * row_count : (h + 1) * row_count]
            return carry

        lax.fori_loop(0, tile_count, put, 0)


def attention(counts, tiles, kv, qg, ld, out_dtype):
    blocks, _, span, width = kv.shape
    sources, _, row_count, lanes = qg.shape
    per_tile = TILE // row_count
    tile_count = sources // per_tile
    whole = lambda shape: pl.BlockSpec(shape, lambda b, *_: (0,) * len(shape))
    return pl.pallas_call(
        functools.partial(attention_kernel, blocks, tile_count, per_tile),
        out_shape=(
            jax.ShapeDtypeStruct(kv.shape, out_dtype),
            jax.ShapeDtypeStruct((sources, row_count, lanes), jnp.bfloat16),
        ),
        grid_spec=pltpu.PrefetchScalarGridSpec(
            num_scalar_prefetch=2,
            grid=(blocks,),
            in_specs=[
                pl.BlockSpec((1, 2, span, width), lambda b, *_: (b, 0, 0, 0)),
                whole(qg.shape),
                whole(ld.shape),
            ],
            out_specs=(
                pl.BlockSpec((1, 2, span, width), lambda b, *_: (b, 0, 0, 0)),
                whole((sources, row_count, lanes)),
            ),
            scratch_shapes=[
                pltpu.VMEM((span, width), jnp.float32),
                pltpu.VMEM((span, width), jnp.float32),
                pltpu.VMEM((tile_count, width, lanes), jnp.float32),
            ],
        ),
        compiler_params=pltpu.CompilerParams(vmem_limit_bytes=48 * 2**20),
        cost_estimate=pl.CostEstimate(
            flops=2 * blocks * span * width * lanes * tile_count * 5 // 2,
            bytes_accessed=16 * 2**20,
            transcendentals=blocks * span * lanes * tile_count // 2,
        ),
        name="attention",
    )(counts, tiles, kv, qg, ld)


def routes(kind, devices, slices, me):
    layers = devices // slices
    j, z = lax.rem(me, slices), me // slices
    base = me - j
    if kind in ("all", "cast"):

        def step(r):
            target = lax.rem(me + r, devices)
            return target, (target if kind == "all" else lax.rem(target, slices)), me

        return devices, step
    if kind == "layer":

        def step(r):
            other = lax.rem(j + r, slices)
            return base + other, other, j

        return slices, step
    if kind == "z":

        def step(r):
            other = lax.rem(z + r, layers)
            return other * slices + j, other, z

        return layers, step
    quads = slices // 2

    def step(r):
        other = lax.rem(j // 2 + r, quads)
        return base + 2 * other + lax.rem(j, 2), other, j // 2

    return quads, step


def repeat(first, count, body):
    if count - first <= 8:
        for r in range(first, count):
            body(r)
    else:
        lax.fori_loop(first, count, lambda r, c: (body(r), c)[1], 0)


def exchange_kernel(kinds, devices, slices, gathered, *refs):
    n = len(kinds)
    total = n + gathered
    sources, outs = refs[:total], refs[total : 2 * total]
    sems = refs[2 * total :]
    me = lax.axis_index("psg")
    barrier = pltpu.get_barrier_semaphore()
    if "all" in kinds or "cast" in kinds:
        greeted = ("all",)
    else:
        greeted = ("z", "layer")
    count = 0
    for kind in greeted:
        size, step = routes(kind, devices, slices, me)
        count += size - 1

        def greet(r, step=step):
            pl.semaphore_signal(barrier, inc=1, device_id={"psg": step(r)[0]}, device_id_type=pl.DeviceIdType.MESH)

        repeat(1, size, greet)
    pl.semaphore_wait(barrier, count)

    def remote(src, dst, send, recv, target):
        return pltpu.make_async_remote_copy(
            src_ref=src,
            dst_ref=dst,
            send_sem=send,
            recv_sem=recv,
            device_id={"psg": target},
            device_id_type=pl.DeviceIdType.MESH,
        )

    if gathered:
        j, z = lax.rem(me, slices), me // slices
        parity = lax.rem(j, 2)
        partner = me + 1 - 2 * parity
        layers = devices // slices
        mine, pair = sources[n], outs[n]
        send, recv, pair_send, pair_recv, own = sems[3 * n :]
        along = []
        for r in range(1, layers):
            target = lax.rem(z + r, layers) * slices + j
            along.append(remote(mine, pair.at[parity, z], send.at[r], recv.at[r], target))
            along[-1].start()
        across = [remote(mine, pair.at[parity, z], pair_send.at[0], pair_recv.at[0], partner)]
        across[0].start()
        kept = pltpu.make_async_copy(mine, pair.at[parity, z], own)
        kept.start()

    moves, stays = [], []
    for i, kind in enumerate(kinds):
        size, step = routes(kind, devices, slices, me)

        def copy(r, i=i, step=step):
            target, chunk, slot = step(r)
            return remote(
                sources[i].at[chunk], outs[i].at[slot], sems[3 * i].at[r], sems[3 * i + 1].at[r], target
            )

        moves.append((size, copy))
        chunk, slot = step(0)[1:]
        stays.append(pltpu.make_async_copy(sources[i].at[chunk], outs[i].at[slot], sems[3 * i + 2]))
    for size, copy in moves:
        repeat(1, size, lambda r, copy=copy: copy(r).start())
    for stay in stays:
        stay.start()

    if gathered:
        for r in range(1, layers):
            along[r - 1].wait_recv()
            landed = pair.at[parity, lax.rem(z - r + layers, layers)]
            across.append(remote(landed, landed, pair_send.at[r], pair_recv.at[r], partner))
            across[-1].start()
        for copy in along:
            copy.wait_send()
        for copy in across:
            copy.wait()
        kept.wait()
    for stay in stays:
        stay.wait()
    for size, copy in moves:
        repeat(1, size, lambda r, copy=copy: copy(r).wait())


def exchange(name, number, devices, slices, parts, gather=None):
    kinds = tuple(kind for kind, _ in parts)
    arrays = [array for _, array in parts]
    layers = devices // slices
    sizes = {"all": devices, "cast": devices, "layer": slices, "z": layers, "parity": slices // 2}
    shapes = [
        jax.ShapeDtypeStruct((sizes[kind],) + array.shape[1:], array.dtype) for kind, array in parts
    ]
    scratch = []
    for kind in kinds:
        scratch += [pltpu.SemaphoreType.DMA((sizes[kind],))] * 2 + [pltpu.SemaphoreType.DMA]
    if gather is not None:
        arrays.append(gather)
        shapes.append(jax.ShapeDtypeStruct((2, layers) + gather.shape, gather.dtype))
        scratch += [pltpu.SemaphoreType.DMA((layers,))] * 4 + [pltpu.SemaphoreType.DMA]
    anywhere = pl.BlockSpec(memory_space=pl.ANY)
    return pl.pallas_call(
        functools.partial(exchange_kernel, kinds, devices, slices, int(gather is not None)),
        out_shape=tuple(shapes),
        in_specs=[anywhere] * len(arrays),
        out_specs=tuple([anywhere] * len(shapes)),
        scratch_shapes=scratch,
        compiler_params=pltpu.CompilerParams(collective_id=number, has_side_effects=True),
        cost_estimate=pl.CostEstimate(flops=0, bytes_accessed=60 * 2**20, transcendentals=0),
        name=name,
    )(*arrays)


def send_to(src, dst, send, recv, target):
    return pltpu.make_async_remote_copy(
        src_ref=src,
        dst_ref=dst,
        send_sem=send,
        recv_sem=recv,
        device_id={"psg": target},
        device_id_type=pl.DeviceIdType.MESH,
    )


def inward_kernel(devices, slices, *refs):
    q_ref, g_ref, ld_ref, k_ref, v_ref, qg_out, ld_out, kv_out = refs[:8]
    in_send, in_recv, kv_send, kv_recv, ld_send, ld_recv, up_send, up_recv, down_send, down_recv, own = refs[8:]
    layers = devices // slices
    me = lax.axis_index("psg")
    j, z = lax.rem(me, slices), me // slices
    base = me - j
    lanes, width = q_ref.shape[1] // slices, k_ref.shape[1] // slices
    barrier = pltpu.get_barrier_semaphore()

    def greet(r, c):
        other = lax.rem(me + r, devices)
        pl.semaphore_signal(barrier, inc=1, device_id={"psg": other}, device_id_type=pl.DeviceIdType.MESH)
        return c

    lax.fori_loop(1, devices, greet, 0)
    pl.semaphore_wait(barrier, devices - 1)

    def columns(ref, part, size):
        return ref.at[:, pl.ds(pl.multiple_of(part * size, size), size)]

    def inside(r):
        other = lax.rem(j + r, slices)
        return [
            send_to(columns(ref, other, lanes), qg_out.at[me, i], in_send.at[i, r], in_recv.at[i, r], base + other)
            for i, ref in enumerate((q_ref, g_ref))
        ]

    def passages(r):
        other = lax.rem(j + r, slices)
        return [
            send_to(columns(ref, other, width), kv_out.at[j, i], kv_send.at[i, r], kv_recv.at[i, r], base + other)
            for i, ref in enumerate((k_ref, v_ref))
        ]

    def small(r):
        other = lax.rem(me + r, devices)
        return send_to(ld_ref.at[lax.rem(other, slices)], ld_out.at[me], ld_send.at[r], ld_recv.at[r], other)

    def hop(sent, r, up):
        layer = z - sent if up else z + sent
        source = layer * slices + lax.rem(j - r + slices, slices)
        ref = qg_out.at[source]
        if up:
            return send_to(ref, ref, up_send.at[sent, r], up_recv.at[sent, r], me + slices)
        return send_to(ref, ref, down_send.at[sent, r], down_recv.at[sent, r], me - slices)

    def hop_here(sent, r, up):
        layer = z - sent - 1 if up else z + sent + 1
        source = layer * slices + lax.rem(j - r + slices, slices)
        ref = qg_out.at[source]
        if up:
            return send_to(ref, ref, up_send.at[sent, r], up_recv.at[sent, r], lax.rem(me + 1, devices))
        return send_to(ref, ref, down_send.at[sent, r], down_recv.at[sent, r], lax.rem(me + 1, devices))

    kept = [
        pltpu.make_async_copy(columns(q_ref, j, lanes), qg_out.at[me, 0], own.at[0]),
        pltpu.make_async_copy(columns(g_ref, j, lanes), qg_out.at[me, 1], own.at[1]),
        pltpu.make_async_copy(columns(k_ref, j, width), kv_out.at[j, 0], own.at[2]),
        pltpu.make_async_copy(columns(v_ref, j, width), kv_out.at[j, 1], own.at[3]),
        pltpu.make_async_copy(ld_ref.at[j], ld_out.at[me], own.at[4]),
    ]
    for copy in kept:
        copy.start()
    for r in range(1, slices):
        for copy in inside(r):
            copy.start()
    for copy in kept:
        copy.wait()

    def forward(sent, r):
        @pl.when((z < layers - 1) & (z >= sent))
        def _():
            hop(sent, r, True).start()

        @pl.when((z > 0) & (z + sent < layers))
        def _():
            hop(sent, r, False).start()

    forward(0, 0)

    def first(r, c):
        for copy in inside(r):
            copy.wait_recv()
        forward(0, r)
        return c

    lax.fori_loop(1, slices, first, 0)
    for r in range(1, slices):
        for copy in passages(r):
            copy.start()
    lax.fori_loop(1, devices, lambda r, c: (small(r).start(), c)[1], 0)

    def later(n, c):
        sent, r = n // slices, lax.rem(n, slices)

        @pl.when(z > sent)
        def _():
            hop_here(sent, r, True).wait_recv()

        @pl.when((z > sent) & (z < layers - 1))
        def _():
            hop(sent + 1, r, True).start()

        @pl.when(z + sent + 1 < layers)
        def _():
            hop_here(sent, r, False).wait_recv()

        @pl.when((z + sent + 1 < layers) & (z > 0))
        def _():
            hop(sent + 1, r, False).start()

        return c

    lax.fori_loop(0, (layers - 1) * slices, later, 0)

    for r in range(1, slices):
        for copy in inside(r):
            copy.wait_send()
        for copy in passages(r):
            copy.wait()
    lax.fori_loop(1, devices, lambda r, c: (small(r).wait(), c)[1], 0)

    def ended(n, c):
        sent, r = n // slices, lax.rem(n, slices)

        @pl.when((z < layers - 1) & (z >= sent))
        def _():
            hop(sent, r, True).wait_send()

        @pl.when((z > 0) & (z + sent < layers))
        def _():
            hop(sent, r, False).wait_send()

        return c

    lax.fori_loop(0, (layers - 1) * slices, ended, 0)


def inward(devices, slices, queries, grad_out, ld, keys, values):
    layers = devices // slices
    row_count, columns = queries.shape
    span = keys.shape[0]
    dma = pltpu.SemaphoreType.DMA
    anywhere = pl.BlockSpec(memory_space=pl.ANY)
    return pl.pallas_call(
        functools.partial(inward_kernel, devices, slices),
        out_shape=(
            jax.ShapeDtypeStruct((devices, 2, row_count, columns // slices), queries.dtype),
            jax.ShapeDtypeStruct((devices,) + ld.shape[1:], ld.dtype),
            jax.ShapeDtypeStruct((slices, 2, span, keys.shape[1] // slices), keys.dtype),
        ),
        in_specs=[anywhere] * 5,
        out_specs=(anywhere,) * 3,
        scratch_shapes=[dma((2, slices))] * 4
        + [dma((devices,))] * 2
        + [dma((layers, slices))] * 4
        + [dma((5,))],
        compiler_params=pltpu.CompilerParams(collective_id=0, has_side_effects=True),
        cost_estimate=pl.CostEstimate(flops=0, bytes_accessed=60 * 2**20, transcendentals=0),
        name="exchange_in",
    )(queries, grad_out, ld, keys, values)


def finish_kernel(slices, dkv_ref, hidden_ref, dk_ref, dv_ref, out_ref):
    step = pl.program_id(0)
    dk_ref[...] = dkv_ref[0, 0].astype(jnp.float32)
    dv_ref[...] = dkv_ref[0, 1].astype(jnp.float32)
    quads = slices // 2
    width = hidden_ref.shape[-1] // quads
    layers = hidden_ref.shape[0]

    @pl.when(step < 2 * layers)
    def _():
        z, parity = step // 2, lax.rem(step, 2)
        total = hidden_ref[z, 0, parity].astype(jnp.float32)
        for k in range(1, quads):
            total += hidden_ref[z, k, parity].astype(jnp.float32)
        for k in range(quads):
            first = (z * slices + 2 * k + parity) * width
            out_ref[:, pl.ds(pl.multiple_of(first, width), width)] = total[:, k * width : (k + 1) * width]


def finish(slices, dkv, hidden):
    _, _, span, width = dkv.shape
    layers, quads, _, row_count, part = hidden.shape
    out = jax.ShapeDtypeStruct((span, slices * width), jnp.float32)
    return pl.pallas_call(
        functools.partial(finish_kernel, slices),
        out_shape=(out, out, jax.ShapeDtypeStruct((row_count, layers * 2 * part), jnp.float32)),
        grid=(max(slices, 2 * layers),),
        in_specs=[
            pl.BlockSpec((1, 2, span, width), lambda s: (jnp.minimum(s, slices - 1), 0, 0, 0)),
            pl.BlockSpec(hidden.shape, lambda s: (0, 0, 0, 0, 0)),
        ],
        out_specs=(
            pl.BlockSpec((span, width), lambda s: (0, jnp.minimum(s, slices - 1))),
            pl.BlockSpec((span, width), lambda s: (0, jnp.minimum(s, slices - 1))),
            pl.BlockSpec((row_count, layers * 2 * part), lambda s: (0, 0)),
        ),
        cost_estimate=pl.CostEstimate(flops=0, bytes_accessed=8 * 2**20, transcendentals=0),
        name="finish",
    )(dkv, hidden)


def on_device(queries, grad_out, attn_out, log_sum, keys, values, proj_weight, attend, qlen):
    row_count, columns = queries.shape
    head_count = log_sum.shape[0]
    slices = head_count // GROUP
    span = keys.shape[0]
    devices = lax.axis_size("psg")
    layers = devices // slices
    me = lax.axis_index("psg")
    lanes = GROUP * ATTN_WIDTH
    wide = GROUP * row_count
    tile_count = devices * row_count // TILE
    run = functools.partial(exchange, devices=devices, slices=slices)

    products = grad_out.astype(jnp.float32) * attn_out.astype(jnp.float32)
    delta = jnp.sum(products.reshape(row_count, head_count, ATTN_WIDTH), axis=2).T
    ld = jnp.stack([log_sum * LOG2_E, delta])
    ld = ld.reshape(2, slices, wide).transpose(1, 0, 2)
    if slices > 1:
        qg, ld, kv = inward(devices, slices, queries, grad_out, ld, keys, values)
    else:
        kv = jnp.stack([keys, values])[None]
        qg = jnp.stack([queries, grad_out])[None]
        qg, ld = run("exchange_in", 0, parts=[("cast", qg), ("cast", ld)])

    block_ids = (me // slices) * slices + jnp.arange(slices, dtype=jnp.int32)
    named = jnp.any(attend[None] == block_ids[:, None, None], axis=2)
    tile_ids = jnp.arange(tile_count, dtype=jnp.int32)
    tile_start = tile_ids * TILE % PADDED_ASK_LEN
    tile_live = tile_start < jnp.repeat(qlen, PADDED_ASK_LEN // TILE)
    live = jnp.repeat(named, PADDED_ASK_LEN // TILE, axis=1) & tile_live[None]
    rank = jnp.cumsum(live.astype(jnp.int32), axis=1) - 1
    chosen = live[:, None, :] & (rank[:, None, :] == tile_ids[None, :, None])
    tiles = jnp.sum(jnp.where(chosen, tile_ids[None, None, :], 0), axis=2).astype(jnp.int32)
    counts = jnp.sum(live.astype(jnp.int32), axis=1)

    out_dtype = jnp.bfloat16 if slices > 1 else jnp.float32
    dkv, dq = attention(counts, tiles, kv, qg, ld, out_dtype)

    dq = dq.reshape(layers, slices, row_count, lanes)
    if slices > 1:
        dq, dkv = run("exchange_terms", 1, parts=[("z", dq), ("layer", dkv)])
    else:
        (dq,) = run("exchange_terms", 1, parts=[("all", dq)])
    summed = jnp.sum(dq.astype(jnp.float32), axis=0)
    low = summed.astype(jnp.bfloat16).reshape(slices * row_count, lanes)

    out_columns = proj_weight.shape[0]
    if slices > 1:
        weight = proj_weight.reshape(out_columns, slices // 2, 2 * lanes).transpose(1, 0, 2)
        summed, weight, low = run(
            "exchange_rows", 2, parts=[("layer", summed), ("parity", weight)], gather=low
        )
        low = low.reshape(2, devices * row_count, lanes)
        weight = weight.reshape(slices // 2 * out_columns, 2 * lanes)
        hidden = dot(low[0], weight[:, :lanes], NT) + dot(low[1], weight[:, lanes:], NT)
        hidden = hidden.astype(jnp.bfloat16).reshape(devices, row_count, slices // 2 * out_columns)
        (hidden,) = run("exchange_hidden", 3, parts=[("all", hidden)])
        hidden = hidden.reshape(layers, slices // 2, 2, row_count, slices // 2 * out_columns)
        grad_keys, grad_values, hidden = finish(slices, dkv, hidden)
    else:
        all_low = lax.all_gather(low, "psg", axis=0, tiled=True)
        hidden = dot(all_low, proj_weight, NT)
        hidden = lax.all_to_all(hidden.reshape(devices, row_count, out_columns), "psg", 0, 0)
        hidden = hidden.transpose(1, 0, 2).reshape(row_count, devices * out_columns)
        grad_keys, grad_values = dkv[0, 0], dkv[0, 1]
    grad_hidden = lax.psum(hidden, "qry")
    grad_query = summed.transpose(1, 0, 2).reshape(row_count, columns)
    return (grad_query, grad_keys, grad_values, grad_hidden)


def solution(mesh):
    in_specs = (
        P("psg", "qry"),
        P("psg", "qry"),
        P("psg", "qry"),
        P("qry", "psg"),
        P("psg", "qry"),
        P("psg", "qry"),
        P("psg", "qry"),
        P(),
        P(),
    )
    out_specs = (P("psg", "qry"), P("psg", "qry"), P("psg", "qry"), P("psg", None))
    return jax.shard_map(
        on_device, mesh=mesh, in_specs=in_specs, out_specs=out_specs, check_vma=False
    )
```

```python
import functools

import jax
import jax.numpy as jnp
from jax import lax
from jax.experimental import pallas as pl
from jax.experimental.pallas import tpu as pltpu
from jax.sharding import PartitionSpec as P

ATTN_WIDTH = 128
GROUP = 4
PADDED_ASK_LEN = 256
TILE = 128
LOG2_E = 1.4426950408889634
SCALE = ATTN_WIDTH ** (-0.5)
NT = (((1,), (1,)), ((), ()))
NN = (((1,), (0,)), ((), ()))


def dot(a, b, dims=NN):
    return lax.dot_general(a, b, dims, preferred_element_type=jnp.float32)


def head_rows(qg_ref, first, per_part, which):
    pieces = [
        qg_ref[first + k, which, :, h * ATTN_WIDTH : (h + 1) * ATTN_WIDTH]
        for k in range(per_part)
        for h in range(GROUP)
    ]
    return jnp.concatenate(pieces, axis=0)


def attention_kernel(
    blocks, tile_count, per_tile, counts, tiles, kv_ref, qg_ref, ld_ref, dkv_ref, dq_ref, dk_acc, dv_acc, dq_acc
):
    block = pl.program_id(0)
    per_part = per_tile // 2
    row_count = TILE // per_tile
    wide = GROUP * row_count

    @pl.when(block == 0)
    def _():
        dq_acc[...] = jnp.zeros_like(dq_acc)

    dk_acc[...] = jnp.zeros_like(dk_acc)
    dv_acc[...] = jnp.zeros_like(dv_acc)
    key_rows_t = kv_ref[0, 0].T

    def visit(i, carry):
        tile = tiles[block, i]
        keys, values = kv_ref[0, 0], kv_ref[0, 1]
        dk, dv = None, None
        for part in range(2):
            rows = slice(part * 256, part * 256 + 256)
            first = tile * per_tile + part * per_part
            q = head_rows(qg_ref, first, per_part, 0)
            g = head_rows(qg_ref, first, per_part, 1)
            ld = jnp.concatenate([ld_ref[first + k] for k in range(per_part)], axis=1)
            lse, delta = ld[0:1], ld[1:2]
            prob = jnp.exp2(dot(keys, q, NT) * (SCALE * LOG2_E) - lse)
            dprob = dot(values, g, NT)
            dscore = (prob * (dprob - delta)).astype(jnp.bfloat16)
            v_term = dot(prob.astype(jnp.bfloat16), g)
            k_term = dot(dscore, q)
            dv = v_term if dv is None else dv + v_term
            dk = k_term if dk is None else dk + k_term
            dq_acc[tile, :, rows] += dot(key_rows_t, dscore)
        dk_acc[...] += dk
        dv_acc[...] += dv
        return carry

    lax.fori_loop(0, counts[block], visit, 0)
    dkv_ref[0, 0] = (dk_acc[...] * SCALE).astype(dkv_ref.dtype)
    dkv_ref[0, 1] = dv_acc[...].astype(dkv_ref.dtype)

    @pl.when(block == blocks - 1)
    def _():
        def put(tile, carry):
            for k in range(per_tile):
                piece = dq_acc[tile, :, k * wide : (k + 1) * wide] * SCALE
                piece = piece.T.astype(dq_ref.dtype)
                for h in range(GROUP):
                    cols = slice(h * ATTN_WIDTH, (h + 1) * ATTN_WIDTH)
                    dq_ref[tile * per_tile + k, :, cols] = piece[h * row_count : (h + 1) * row_count]
            return carry

        lax.fori_loop(0, tile_count, put, 0)


def attention(counts, tiles, kv, qg, ld, out_dtype):
    blocks, _, span, width = kv.shape
    sources, _, row_count, lanes = qg.shape
    per_tile = TILE // row_count
    tile_count = sources // per_tile
    whole = lambda shape: pl.BlockSpec(shape, lambda b, *_: (0,) * len(shape))
    return pl.pallas_call(
        functools.partial(attention_kernel, blocks, tile_count, per_tile),
        out_shape=(
            jax.ShapeDtypeStruct(kv.shape, out_dtype),
            jax.ShapeDtypeStruct((sources, row_count, lanes), jnp.bfloat16),
        ),
        grid_spec=pltpu.PrefetchScalarGridSpec(
            num_scalar_prefetch=2,
            grid=(blocks,),
            in_specs=[
                pl.BlockSpec((1, 2, span, width), lambda b, *_: (b, 0, 0, 0)),
                whole(qg.shape),
                whole(ld.shape),
            ],
            out_specs=(
                pl.BlockSpec((1, 2, span, width), lambda b, *_: (b, 0, 0, 0)),
                whole((sources, row_count, lanes)),
            ),
            scratch_shapes=[
                pltpu.VMEM((span, width), jnp.float32),
                pltpu.VMEM((span, width), jnp.float32),
                pltpu.VMEM((tile_count, width, lanes), jnp.float32),
            ],
        ),
        compiler_params=pltpu.CompilerParams(vmem_limit_bytes=48 * 2**20),
        cost_estimate=pl.CostEstimate(
            flops=2 * blocks * span * width * lanes * tile_count * 5 // 2,
            bytes_accessed=16 * 2**20,
            transcendentals=blocks * span * lanes * tile_count // 2,
        ),
        name="attention",
    )(counts, tiles, kv, qg, ld)


def routes(kind, devices, slices, me):
    layers = devices // slices
    j, z = lax.rem(me, slices), me // slices
    base = me - j
    if kind in ("all", "cast"):

        def step(r):
            target = lax.rem(me + r, devices)
            return target, (target if kind == "all" else lax.rem(target, slices)), me

        return devices, step
    if kind == "layer":

        def step(r):
            other = lax.rem(j + r, slices)
            return base + other, other, j

        return slices, step
    if kind == "z":

        def step(r):
            other = lax.rem(z + r, layers)
            return other * slices + j, other, z

        return layers, step
    quads = slices // 2

    def step(r):
        other = lax.rem(j // 2 + r, quads)
        return base + 2 * other + lax.rem(j, 2), other, j // 2

    return quads, step


def repeat(first, count, body):
    if count - first <= 8:
        for r in range(first, count):
            body(r)
    else:
        lax.fori_loop(first, count, lambda r, c: (body(r), c)[1], 0)


def exchange_kernel(kinds, devices, slices, gathered, *refs):
    n = len(kinds)
    total = n + gathered
    sources, outs = refs[:total], refs[total : 2 * total]
    sems = refs[2 * total :]
    me = lax.axis_index("psg")
    barrier = pltpu.get_barrier_semaphore()
    if "all" in kinds or "cast" in kinds:
        greeted = ("all",)
    else:
        greeted = ("z", "layer")
    count = 0
    for kind in greeted:
        size, step = routes(kind, devices, slices, me)
        count += size - 1

        def greet(r, step=step):
            pl.semaphore_signal(barrier, inc=1, device_id={"psg": step(r)[0]}, device_id_type=pl.DeviceIdType.MESH)

        repeat(1, size, greet)
    pl.semaphore_wait(barrier, count)

    def remote(src, dst, send, recv, target):
        return pltpu.make_async_remote_copy(
            src_ref=src,
            dst_ref=dst,
            send_sem=send,
            recv_sem=recv,
            device_id={"psg": target},
            device_id_type=pl.DeviceIdType.MESH,
        )

    if gathered:
        j, z = lax.rem(me, slices), me // slices
        parity = lax.rem(j, 2)
        partner = me + 1 - 2 * parity
        layers = devices // slices
        mine, pair = sources[n], outs[n]
        send, recv, pair_send, pair_recv, own = sems[3 * n :]
        along = []
        for r in range(1, layers):
            target = lax.rem(z + r, layers) * slices + j
            along.append(remote(mine, pair.at[parity, z], send.at[r], recv.at[r], target))
            along[-1].start()
        across = [remote(mine, pair.at[parity, z], pair_send.at[0], pair_recv.at[0], partner)]
        across[0].start()
        kept = pltpu.make_async_copy(mine, pair.at[parity, z], own)
        kept.start()

    moves, stays = [], []
    for i, kind in enumerate(kinds):
        size, step = routes(kind, devices, slices, me)

        def copy(r, i=i, step=step):
            target, chunk, slot = step(r)
            return remote(
                sources[i].at[chunk], outs[i].at[slot], sems[3 * i].at[r], sems[3 * i + 1].at[r], target
            )

        moves.append((size, copy))
        chunk, slot = step(0)[1:]
        stays.append(pltpu.make_async_copy(sources[i].at[chunk], outs[i].at[slot], sems[3 * i + 2]))
    for size, copy in moves:
        repeat(1, size, lambda r, copy=copy: copy(r).start())
    for stay in stays:
        stay.start()

    if gathered:
        for r in range(1, layers):
            along[r - 1].wait_recv()
            landed = pair.at[parity, lax.rem(z - r + layers, layers)]
            across.append(remote(landed, landed, pair_send.at[r], pair_recv.at[r], partner))
            across[-1].start()
        for copy in along:
            copy.wait_send()
        for copy in across:
            copy.wait()
        kept.wait()
    for stay in stays:
        stay.wait()
    for size, copy in moves:
        repeat(1, size, lambda r, copy=copy: copy(r).wait())


def exchange(name, number, devices, slices, parts, gather=None):
    kinds = tuple(kind for kind, _ in parts)
    arrays = [array for _, array in parts]
    layers = devices // slices
    sizes = {"all": devices, "cast": devices, "layer": slices, "z": layers, "parity": slices // 2}
    shapes = [
        jax.ShapeDtypeStruct((sizes[kind],) + array.shape[1:], array.dtype) for kind, array in parts
    ]
    scratch = []
    for kind in kinds:
        scratch += [pltpu.SemaphoreType.DMA((sizes[kind],))] * 2 + [pltpu.SemaphoreType.DMA]
    if gather is not None:
        arrays.append(gather)
        shapes.append(jax.ShapeDtypeStruct((2, layers) + gather.shape, gather.dtype))
        scratch += [pltpu.SemaphoreType.DMA((layers,))] * 4 + [pltpu.SemaphoreType.DMA]
    anywhere = pl.BlockSpec(memory_space=pl.ANY)
    return pl.pallas_call(
        functools.partial(exchange_kernel, kinds, devices, slices, int(gather is not None)),
        out_shape=tuple(shapes),
        in_specs=[anywhere] * len(arrays),
        out_specs=tuple([anywhere] * len(shapes)),
        scratch_shapes=scratch,
        compiler_params=pltpu.CompilerParams(collective_id=number, has_side_effects=True),
        cost_estimate=pl.CostEstimate(flops=0, bytes_accessed=60 * 2**20, transcendentals=0),
        name=name,
    )(*arrays)


def send_to(src, dst, send, recv, target):
    return pltpu.make_async_remote_copy(
        src_ref=src,
        dst_ref=dst,
        send_sem=send,
        recv_sem=recv,
        device_id={"psg": target},
        device_id_type=pl.DeviceIdType.MESH,
    )


def inward_kernel(devices, slices, *refs):
    q_ref, g_ref, ld_ref, k_ref, v_ref, qg_out, ld_out, kv_out = refs[:8]
    in_send, in_recv, kv_send, kv_recv, ld_send, ld_recv, up_send, up_recv, down_send, down_recv, own = refs[8:]
    layers = devices // slices
    me = lax.axis_index("psg")
    j, z = lax.rem(me, slices), me // slices
    base = me - j
    lanes, width = q_ref.shape[1] // slices, k_ref.shape[1] // slices
    barrier = pltpu.get_barrier_semaphore()

    def greet(r, c):
        other = lax.rem(me + r, devices)
        pl.semaphore_signal(barrier, inc=1, device_id={"psg": other}, device_id_type=pl.DeviceIdType.MESH)
        return c

    lax.fori_loop(1, devices, greet, 0)
    pl.semaphore_wait(barrier, devices - 1)

    def columns(ref, part, size):
        return ref.at[:, pl.ds(pl.multiple_of(part * size, size), size)]

    def inside(r):
        other = lax.rem(j + r, slices)
        return [
            send_to(columns(ref, other, lanes), qg_out.at[me, i], in_send.at[i, r], in_recv.at[i, r], base + other)
            for i, ref in enumerate((q_ref, g_ref))
        ]

    def passages(r):
        other = lax.rem(j + r, slices)
        return [
            send_to(columns(ref, other, width), kv_out.at[j, i], kv_send.at[i, r], kv_recv.at[i, r], base + other)
            for i, ref in enumerate((k_ref, v_ref))
        ]

    def small(r):
        other = lax.rem(me + r, devices)
        return send_to(ld_ref.at[lax.rem(other, slices)], ld_out.at[me], ld_send.at[r], ld_recv.at[r], other)

    def hop(sent, r, up):
        layer = z - sent if up else z + sent
        source = layer * slices + lax.rem(j - r + slices, slices)
        ref = qg_out.at[source]
        if up:
            return send_to(ref, ref, up_send.at[sent, r], up_recv.at[sent, r], me + slices)
        return send_to(ref, ref, down_send.at[sent, r], down_recv.at[sent, r], me - slices)

    def hop_here(sent, r, up):
        layer = z - sent - 1 if up else z + sent + 1
        source = layer * slices + lax.rem(j - r + slices, slices)
        ref = qg_out.at[source]
        if up:
            return send_to(ref, ref, up_send.at[sent, r], up_recv.at[sent, r], lax.rem(me + 1, devices))
        return send_to(ref, ref, down_send.at[sent, r], down_recv.at[sent, r], lax.rem(me + 1, devices))

    kept = [
        pltpu.make_async_copy(columns(q_ref, j, lanes), qg_out.at[me, 0], own.at[0]),
        pltpu.make_async_copy(columns(g_ref, j, lanes), qg_out.at[me, 1], own.at[1]),
        pltpu.make_async_copy(columns(k_ref, j, width), kv_out.at[j, 0], own.at[2]),
        pltpu.make_async_copy(columns(v_ref, j, width), kv_out.at[j, 1], own.at[3]),
        pltpu.make_async_copy(ld_ref.at[j], ld_out.at[me], own.at[4]),
    ]
    for copy in kept:
        copy.start()
    for r in range(1, slices):
        for copy in inside(r):
            copy.start()
    for copy in kept:
        copy.wait()

    def forward(sent, r):
        @pl.when((z < layers - 1) & (z >= sent))
        def _():
            hop(sent, r, True).start()

        @pl.when((z > 0) & (z + sent < layers))
        def _():
            hop(sent, r, False).start()

    forward(0, 0)

    def first(r, c):
        for copy in inside(r):
            copy.wait_recv()
        forward(0, r)
        return c

    lax.fori_loop(1, slices, first, 0)
    for r in range(1, slices):
        for copy in passages(r):
            copy.start()
    lax.fori_loop(1, devices, lambda r, c: (small(r).start(), c)[1], 0)

    def later(n, c):
        sent, r = n // slices, lax.rem(n, slices)

        @pl.when(z > sent)
        def _():
            hop_here(sent, r, True).wait_recv()

        @pl.when((z > sent) & (z < layers - 1))
        def _():
            hop(sent + 1, r, True).start()

        @pl.when(z + sent + 1 < layers)
        def _():
            hop_here(sent, r, False).wait_recv()

        @pl.when((z + sent + 1 < layers) & (z > 0))
        def _():
            hop(sent + 1, r, False).start()

        return c

    lax.fori_loop(0, (layers - 1) * slices, later, 0)

    for r in range(1, slices):
        for copy in inside(r):
            copy.wait_send()
        for copy in passages(r):
            copy.wait()
    lax.fori_loop(1, devices, lambda r, c: (small(r).wait(), c)[1], 0)

    def ended(n, c):
        sent, r = n // slices, lax.rem(n, slices)

        @pl.when((z < layers - 1) & (z >= sent))
        def _():
            hop(sent, r, True).wait_send()

        @pl.when((z > 0) & (z + sent < layers))
        def _():
            hop(sent, r, False).wait_send()

        return c

    lax.fori_loop(0, (layers - 1) * slices, ended, 0)


def inward(devices, slices, queries, grad_out, ld, keys, values):
    layers = devices // slices
    row_count, columns = queries.shape
    span = keys.shape[0]
    dma = pltpu.SemaphoreType.DMA
    anywhere = pl.BlockSpec(memory_space=pl.ANY)
    return pl.pallas_call(
        functools.partial(inward_kernel, devices, slices),
        out_shape=(
            jax.ShapeDtypeStruct((devices, 2, row_count, columns // slices), queries.dtype),
            jax.ShapeDtypeStruct((devices,) + ld.shape[1:], ld.dtype),
            jax.ShapeDtypeStruct((slices, 2, span, keys.shape[1] // slices), keys.dtype),
        ),
        in_specs=[anywhere] * 5,
        out_specs=(anywhere,) * 3,
        scratch_shapes=[dma((2, slices))] * 4
        + [dma((devices,))] * 2
        + [dma((layers, slices))] * 4
        + [dma((5,))],
        compiler_params=pltpu.CompilerParams(collective_id=0, has_side_effects=True),
        cost_estimate=pl.CostEstimate(flops=0, bytes_accessed=60 * 2**20, transcendentals=0),
        name="exchange_in",
    )(queries, grad_out, ld, keys, values)


def outward_kernel(devices, slices, dq_ref, dkv_ref, w_ref, gq_out, dkv_out, hid_out, *scratch):
    terms, summed, pair, weight, hidden = scratch[:5]
    term_send, term_recv, up_send, up_recv, down_send, down_recv, pair_send, pair_recv = scratch[5:13]
    w_send, w_recv, dkv_send, dkv_recv, gq_send, gq_recv, hid_send, hid_recv, own = scratch[13:]
    layers = devices // slices
    quads = slices // 2
    me = lax.axis_index("psg")
    j, z = lax.rem(me, slices), me // slices
    base = me - j
    parity = lax.rem(j, 2)
    partner = me + 1 - 2 * parity
    row_count, lanes = dq_ref.shape[2:]
    chunk_rows = 2 * row_count
    barrier = pltpu.get_barrier_semaphore()

    def greet(r, c):
        other = lax.rem(me + r, devices)
        pl.semaphore_signal(barrier, inc=1, device_id={"psg": other}, device_id_type=pl.DeviceIdType.MESH)
        return c

    lax.fori_loop(1, devices, greet, 0)
    pl.semaphore_wait(barrier, devices - 1)

    def term(c, r, here=False):
        other = lax.rem(z + r, layers)
        slot = lax.rem(z - r + layers, layers) if here else z
        devs = slice(2 * c, 2 * c + 2)
        return send_to(
            dq_ref.at[other, devs], terms.at[slot, devs], term_send.at[c, r], term_recv.at[c, r],
            other * slices + j,
        )

    def weights(r):
        other = lax.rem(j // 2 + r, quads)
        width = 2 * lanes
        source = w_ref.at[:, pl.ds(pl.multiple_of(other * width, width), width)]
        if r == 0:
            return pltpu.make_async_copy(source, weight.at[j // 2], own.at[0])
        return send_to(
            source, weight.at[j // 2], w_send.at[r], w_recv.at[r], base + 2 * other + parity
        )

    def passages(r):
        other = lax.rem(j + r, slices)
        if r == 0:
            return pltpu.make_async_copy(dkv_ref.at[other], dkv_out.at[j], own.at[1])
        return send_to(dkv_ref.at[other], dkv_out.at[j], dkv_send.at[r], dkv_recv.at[r], base + other)

    def rows(r):
        other = lax.rem(j + r, slices)
        if r == 0:
            return pltpu.make_async_copy(summed.at[other], gq_out.at[j], own.at[2])
        return send_to(summed.at[other], gq_out.at[j], gq_send.at[r], gq_recv.at[r], base + other)

    def piece(core, layer, c):
        return pair.at[core, layer, c * chunk_rows : (c + 1) * chunk_rows]

    def hop(sent, c, up):
        ref = piece(parity, z - sent if up else z + sent, c)
        if up:
            return send_to(ref, ref, up_send.at[sent, c], up_recv.at[sent, c], me + slices)
        return send_to(ref, ref, down_send.at[sent, c], down_recv.at[sent, c], me - slices)

    def hop_here(sent, c, up):
        ref = piece(parity, z - sent - 1 if up else z + sent + 1, c)
        other = lax.rem(me + 1, devices)
        if up:
            return send_to(ref, ref, up_send.at[sent, c], up_recv.at[sent, c], other)
        return send_to(ref, ref, down_send.at[sent, c], down_recv.at[sent, c], other)

    def across(layer, c, here=False):
        ref = piece(1 - parity if here else parity, layer, c)
        return send_to(ref, ref, pair_send.at[layer, c], pair_recv.at[layer, c], partner)

    def columns(layer, r):
        other = lax.rem(j + r, slices)
        target = layer * slices + other
        step = lax.rem(target - me + devices, devices)
        return send_to(
            hidden.at[layer, other], hid_out.at[me], hid_send.at[step], hid_recv.at[step], target
        )

    def product(layer):
        for c in range(quads):
            across(layer, c, True).wait_recv()
        matrix = weight[...].reshape(-1, 2 * lanes)
        out = dot(pair[0, layer], matrix[:, :lanes], NT) + dot(pair[1, layer], matrix[:, lanes:], NT)
        hidden[layer] = out.astype(hidden.dtype).reshape(hidden.shape[1:])

    for c in range(quads):
        for r in range(1, layers):
            term(c, r).start()
    for r in range(quads):
        weights(r).start()
    for r in range(slices):
        passages(r).start()

    for c in range(quads):
        devs = slice(2 * c, 2 * c + 2)
        total = dq_ref[z, devs].astype(jnp.float32)
        for r in range(1, layers):
            term(c, r, True).wait_recv()
            total += terms[lax.rem(z - r + layers, layers), devs].astype(jnp.float32)
        summed[devs] = total
        pair[parity, z, c * chunk_rows : (c + 1) * chunk_rows] = total.astype(pair.dtype).reshape(
            chunk_rows, lanes
        )

        @pl.when(z < layers - 1)
        def _():
            hop(0, c, True).start()

        @pl.when(z > 0)
        def _():
            hop(0, c, False).start()

        across(z, c).start()

    for r in range(1, quads):
        weights(r).wait_recv()
    weights(0).wait()
    product(z)
    for r in range(1, slices):
        columns(z, r).start()
    kept = pltpu.make_async_copy(hidden.at[z, j], hid_out.at[me], own.at[3])
    kept.start()
    for r in range(slices):
        rows(r).start()

    for sent in range(layers - 1):
        for c in range(quads):

            @pl.when(z > sent)
            def _():
                hop_here(sent, c, True).wait_recv()
                across(z - sent - 1, c).start()

            @pl.when((z > sent) & (z < layers - 1))
            def _():
                hop(sent + 1, c, True).start()

            @pl.when(z + sent + 1 < layers)
            def _():
                hop_here(sent, c, False).wait_recv()
                across(z + sent + 1, c).start()

            @pl.when((z + sent + 1 < layers) & (z > 0))
            def _():
                hop(sent + 1, c, False).start()

        @pl.when(z > sent)
        def _():
            product(z - sent - 1)
            for r in range(slices):
                columns(z - sent - 1, r).start()

        @pl.when(z + sent + 1 < layers)
        def _():
            product(z + sent + 1)
            for r in range(slices):
                columns(z + sent + 1, r).start()

    for c in range(quads):
        for r in range(1, layers):
            term(c, r).wait_send()
        for layer in range(layers):
            across(layer, c).wait_send()
        for sent in range(layers - 1):

            @pl.when((z < layers - 1) & (z >= sent))
            def _():
                hop(sent, c, True).wait_send()

            @pl.when((z > 0) & (z + sent < layers))
            def _():
                hop(sent, c, False).wait_send()

    for r in range(1, quads):
        weights(r).wait_send()
    for r in range(slices):
        passages(r).wait()
        rows(r).wait()
    kept.wait()

    def arrived(r, c):
        target = lax.rem(me + r, devices)
        send_to(
            hidden.at[target // slices, lax.rem(target, slices)],
            hid_out.at[lax.rem(me - r + devices, devices)],
            hid_send.at[r],
            hid_recv.at[r],
            target,
        ).wait()
        return c

    lax.fori_loop(1, devices, arrived, 0)


def outward(devices, slices, dq, dkv, weight):
    layers, quads = devices // slices, slices // 2
    _, _, row_count, lanes = dq.shape
    out_columns = weight.shape[0]
    dma = pltpu.SemaphoreType.DMA
    anywhere = pl.BlockSpec(memory_space=pl.ANY)
    return pl.pallas_call(
        functools.partial(outward_kernel, devices, slices),
        out_shape=(
            jax.ShapeDtypeStruct((slices, row_count, lanes), jnp.float32),
            jax.ShapeDtypeStruct(dkv.shape, dkv.dtype),
            jax.ShapeDtypeStruct((devices, row_count, quads * out_columns), jnp.bfloat16),
        ),
        in_specs=[pl.BlockSpec(memory_space=pltpu.VMEM), anywhere, anywhere],
        out_specs=(anywhere,) * 3,
        scratch_shapes=[
            pltpu.VMEM(dq.shape, dq.dtype),
            pltpu.VMEM((slices, row_count, lanes), jnp.float32),
            pltpu.VMEM((2, layers, slices * row_count, lanes), jnp.bfloat16),
            pltpu.VMEM((quads, out_columns, 2 * lanes), weight.dtype),
            pltpu.VMEM((layers, slices, row_count, quads * out_columns), jnp.bfloat16),
        ]
        + [dma((quads, layers))] * 2
        + [dma((layers, quads))] * 6
        + [dma((quads,))] * 2
        + [dma((slices,))] * 4
        + [dma((devices,))] * 2
        + [dma((4,))],
        compiler_params=pltpu.CompilerParams(
            collective_id=1, has_side_effects=True, vmem_limit_bytes=40 * 2**20
        ),
        cost_estimate=pl.CostEstimate(flops=2 * 2**29, bytes_accessed=60 * 2**20, transcendentals=0),
        name="exchange_out",
    )(dq, dkv, weight)


def finish_kernel(slices, dkv_ref, hidden_ref, dk_ref, dv_ref, out_ref):
    step = pl.program_id(0)
    dk_ref[...] = dkv_ref[0, 0].astype(jnp.float32)
    dv_ref[...] = dkv_ref[0, 1].astype(jnp.float32)
    quads = slices // 2
    width = hidden_ref.shape[-1] // quads
    layers = hidden_ref.shape[0]

    @pl.when(step < 2 * layers)
    def _():
        z, parity = step // 2, lax.rem(step, 2)
        total = hidden_ref[z, 0, parity].astype(jnp.float32)
        for k in range(1, quads):
            total += hidden_ref[z, k, parity].astype(jnp.float32)
        for k in range(quads):
            first = (z * slices + 2 * k + parity) * width
            out_ref[:, pl.ds(pl.multiple_of(first, width), width)] = total[:, k * width : (k + 1) * width]


def finish(slices, dkv, hidden):
    _, _, span, width = dkv.shape
    layers, quads, _, row_count, part = hidden.shape
    out = jax.ShapeDtypeStruct((span, slices * width), jnp.float32)
    return pl.pallas_call(
        functools.partial(finish_kernel, slices),
        out_shape=(out, out, jax.ShapeDtypeStruct((row_count, layers * 2 * part), jnp.float32)),
        grid=(max(slices, 2 * layers),),
        in_specs=[
            pl.BlockSpec((1, 2, span, width), lambda s: (jnp.minimum(s, slices - 1), 0, 0, 0)),
            pl.BlockSpec(hidden.shape, lambda s: (0, 0, 0, 0, 0)),
        ],
        out_specs=(
            pl.BlockSpec((span, width), lambda s: (0, jnp.minimum(s, slices - 1))),
            pl.BlockSpec((span, width), lambda s: (0, jnp.minimum(s, slices - 1))),
            pl.BlockSpec((row_count, layers * 2 * part), lambda s: (0, 0)),
        ),
        cost_estimate=pl.CostEstimate(flops=0, bytes_accessed=8 * 2**20, transcendentals=0),
        name="finish",
    )(dkv, hidden)


def on_device(queries, grad_out, attn_out, log_sum, keys, values, proj_weight, attend, qlen):
    row_count, columns = queries.shape
    head_count = log_sum.shape[0]
    slices = head_count // GROUP
    span = keys.shape[0]
    devices = lax.axis_size("psg")
    layers = devices // slices
    me = lax.axis_index("psg")
    lanes = GROUP * ATTN_WIDTH
    wide = GROUP * row_count
    tile_count = devices * row_count // TILE
    run = functools.partial(exchange, devices=devices, slices=slices)

    products = grad_out.astype(jnp.float32) * attn_out.astype(jnp.float32)
    delta = jnp.sum(products.reshape(row_count, head_count, ATTN_WIDTH), axis=2).T
    ld = jnp.stack([log_sum * LOG2_E, delta])
    ld = ld.reshape(2, slices, wide).transpose(1, 0, 2)
    if slices > 1:
        qg, ld, kv = inward(devices, slices, queries, grad_out, ld, keys, values)
    else:
        kv = jnp.stack([keys, values])[None]
        qg = jnp.stack([queries, grad_out])[None]
        qg, ld = run("exchange_in", 0, parts=[("cast", qg), ("cast", ld)])

    block_ids = (me // slices) * slices + jnp.arange(slices, dtype=jnp.int32)
    named = jnp.any(attend[None] == block_ids[:, None, None], axis=2)
    tile_ids = jnp.arange(tile_count, dtype=jnp.int32)
    tile_start = tile_ids * TILE % PADDED_ASK_LEN
    tile_live = tile_start < jnp.repeat(qlen, PADDED_ASK_LEN // TILE)
    live = jnp.repeat(named, PADDED_ASK_LEN // TILE, axis=1) & tile_live[None]
    rank = jnp.cumsum(live.astype(jnp.int32), axis=1) - 1
    chosen = live[:, None, :] & (rank[:, None, :] == tile_ids[None, :, None])
    tiles = jnp.sum(jnp.where(chosen, tile_ids[None, None, :], 0), axis=2).astype(jnp.int32)
    counts = jnp.sum(live.astype(jnp.int32), axis=1)

    out_dtype = jnp.bfloat16 if slices > 1 else jnp.float32
    dkv, dq = attention(counts, tiles, kv, qg, ld, out_dtype)

    dq = dq.reshape(layers, slices, row_count, lanes)
    out_columns = proj_weight.shape[0]
    if slices > 1:
        summed, dkv, hidden = outward(devices, slices, dq, dkv, proj_weight)
        hidden = hidden.reshape(layers, slices // 2, 2, row_count, slices // 2 * out_columns)
        grad_keys, grad_values, hidden = finish(slices, dkv, hidden)
    else:
        (dq,) = run("exchange_terms", 1, parts=[("all", dq)])
        summed = jnp.sum(dq.astype(jnp.float32), axis=0)
        low = summed.astype(jnp.bfloat16).reshape(row_count, lanes)
        all_low = lax.all_gather(low, "psg", axis=0, tiled=True)
        hidden = dot(all_low, proj_weight, NT)
        hidden = lax.all_to_all(hidden.reshape(devices, row_count, out_columns), "psg", 0, 0)
        hidden = hidden.transpose(1, 0, 2).reshape(row_count, devices * out_columns)
        grad_keys, grad_values = dkv[0, 0], dkv[0, 1]
    grad_hidden = lax.psum(hidden, "qry")
    grad_query = summed.transpose(1, 0, 2).reshape(row_count, columns)
    return (grad_query, grad_keys, grad_values, grad_hidden)


def solution(mesh):
    in_specs = (
        P("psg", "qry"),
        P("psg", "qry"),
        P("psg", "qry"),
        P("qry", "psg"),
        P("psg", "qry"),
        P("psg", "qry"),
        P("psg", "qry"),
        P(),
        P(),
    )
    out_specs = (P("psg", "qry"), P("psg", "qry"), P("psg", "qry"), P("psg", None))
    return jax.shard_map(
        on_device, mesh=mesh, in_specs=in_specs, out_specs=out_specs, check_vma=False
    )
```

```python
import functools

import jax
import jax.numpy as jnp
from jax import lax
from jax.experimental import pallas as pl
from jax.experimental.pallas import tpu as pltpu
from jax.sharding import PartitionSpec as P

ATTN_WIDTH = 128
GROUP = 4
PADDED_ASK_LEN = 256
TILE = 128
LOG2_E = 1.4426950408889634
SCALE = ATTN_WIDTH ** (-0.5)
NT = (((1,), (1,)), ((), ()))
NN = (((1,), (0,)), ((), ()))


def dot(a, b, dims=NN):
    return lax.dot_general(a, b, dims, preferred_element_type=jnp.float32)


def head_rows(qg_ref, first, per_part, which):
    pieces = [
        qg_ref[first + k, which, :, h * ATTN_WIDTH : (h + 1) * ATTN_WIDTH]
        for k in range(per_part)
        for h in range(GROUP)
    ]
    return jnp.concatenate(pieces, axis=0)


def attention_kernel(
    blocks, tile_count, per_tile, attend, qlen, kv_ref, qg_ref, ld_ref, dkv_ref, dq_ref, dk_acc, dv_acc, dq_acc
):
    block = pl.program_id(0)
    per_part = per_tile // 2
    row_count = TILE // per_tile
    wide = GROUP * row_count

    @pl.when(block == 0)
    def _():
        dq_acc[...] = jnp.zeros_like(dq_acc)

    dk_acc[...] = jnp.zeros_like(dk_acc)
    dv_acc[...] = jnp.zeros_like(dv_acc)
    key_rows_t = kv_ref[0, 0].T

    def visit(tile, carry):
        keys, values = kv_ref[0, 0], kv_ref[0, 1]
        dk, dv = None, None
        for part in range(2):
            rows = slice(part * 256, part * 256 + 256)
            first = tile * per_tile + part * per_part
            q = head_rows(qg_ref, first, per_part, 0)
            g = head_rows(qg_ref, first, per_part, 1)
            ld = jnp.concatenate([ld_ref[first + k] for k in range(per_part)], axis=1)
            lse, delta = ld[0:1], ld[1:2]
            prob = jnp.exp2(dot(keys, q, NT) * (SCALE * LOG2_E) - lse)
            dprob = dot(values, g, NT)
            dscore = (prob * (dprob - delta)).astype(jnp.bfloat16)
            v_term = dot(prob.astype(jnp.bfloat16), g)
            k_term = dot(dscore, q)
            dv = v_term if dv is None else dv + v_term
            dk = k_term if dk is None else dk + k_term
            dq_acc[tile, :, rows] += dot(key_rows_t, dscore)
        dk_acc[...] += dk
        dv_acc[...] += dv
        return carry

    mine = lax.axis_index("psg")
    mine = mine - lax.rem(mine, blocks) + block
    questions, named = attend.shape

    def ask(question, carry):
        hits = attend[question, 0] == mine
        for i in range(1, named):
            hits = hits | (attend[question, i] == mine)
        first = question * (PADDED_ASK_LEN // TILE)
        count = jnp.where(hits, qlen[question] // TILE, 0)
        return lax.fori_loop(first, first + count, visit, carry)

    lax.fori_loop(0, questions, ask, 0)
    dkv_ref[0, 0] = (dk_acc[...] * SCALE).astype(dkv_ref.dtype)
    dkv_ref[0, 1] = dv_acc[...].astype(dkv_ref.dtype)

    @pl.when(block == blocks - 1)
    def _():
        def put(tile, carry):
            for k in range(per_tile):
                piece = dq_acc[tile, :, k * wide : (k + 1) * wide] * SCALE
                piece = piece.T.astype(dq_ref.dtype)
                for h in range(GROUP):
                    cols = slice(h * ATTN_WIDTH, (h + 1) * ATTN_WIDTH)
                    dq_ref[tile * per_tile + k, :, cols] = piece[h * row_count : (h + 1) * row_count]
            return carry

        lax.fori_loop(0, tile_count, put, 0)


def attention(attend, qlen, kv, qg, ld, out_dtype):
    blocks, _, span, width = kv.shape
    sources, _, row_count, lanes = qg.shape
    per_tile = TILE // row_count
    tile_count = sources // per_tile
    whole = lambda shape: pl.BlockSpec(shape, lambda b, *_: (0,) * len(shape))
    return pl.pallas_call(
        functools.partial(attention_kernel, blocks, tile_count, per_tile),
        out_shape=(
            jax.ShapeDtypeStruct(kv.shape, out_dtype),
            jax.ShapeDtypeStruct((sources, row_count, lanes), jnp.bfloat16),
        ),
        grid_spec=pltpu.PrefetchScalarGridSpec(
            num_scalar_prefetch=2,
            grid=(blocks,),
            in_specs=[
                pl.BlockSpec((1, 2, span, width), lambda b, *_: (b, 0, 0, 0)),
                whole(qg.shape),
                whole(ld.shape),
            ],
            out_specs=(
                pl.BlockSpec((1, 2, span, width), lambda b, *_: (b, 0, 0, 0)),
                whole((sources, row_count, lanes)),
            ),
            scratch_shapes=[
                pltpu.VMEM((span, width), jnp.float32),
                pltpu.VMEM((span, width), jnp.float32),
                pltpu.VMEM((tile_count, width, lanes), jnp.float32),
            ],
        ),
        compiler_params=pltpu.CompilerParams(vmem_limit_bytes=58 * 2**20),
        cost_estimate=pl.CostEstimate(
            flops=2 * blocks * span * width * lanes * tile_count * 5 // 2,
            bytes_accessed=16 * 2**20,
            transcendentals=blocks * span * lanes * tile_count // 2,
        ),
        name="attention",
    )(attend, qlen, kv, qg, ld)


def routes(kind, devices, slices, me):
    layers = devices // slices
    j, z = lax.rem(me, slices), me // slices
    base = me - j
    if kind in ("all", "cast"):

        def step(r):
            target = lax.rem(me + r, devices)
            return target, (target if kind == "all" else lax.rem(target, slices)), me

        return devices, step
    if kind == "layer":

        def step(r):
            other = lax.rem(j + r, slices)
            return base + other, other, j

        return slices, step
    if kind == "z":

        def step(r):
            other = lax.rem(z + r, layers)
            return other * slices + j, other, z

        return layers, step
    quads = slices // 2

    def step(r):
        other = lax.rem(j // 2 + r, quads)
        return base + 2 * other + lax.rem(j, 2), other, j // 2

    return quads, step


def repeat(first, count, body):
    if count - first <= 8:
        for r in range(first, count):
            body(r)
    else:
        lax.fori_loop(first, count, lambda r, c: (body(r), c)[1], 0)


def exchange_kernel(kinds, devices, slices, gathered, *refs):
    n = len(kinds)
    total = n + gathered
    sources, outs = refs[:total], refs[total : 2 * total]
    sems = refs[2 * total :]
    me = lax.axis_index("psg")
    barrier = pltpu.get_barrier_semaphore()
    if "all" in kinds or "cast" in kinds:
        greeted = ("all",)
    else:
        greeted = ("z", "layer")
    count = 0
    for kind in greeted:
        size, step = routes(kind, devices, slices, me)
        count += size - 1

        def greet(r, step=step):
            pl.semaphore_signal(barrier, inc=1, device_id={"psg": step(r)[0]}, device_id_type=pl.DeviceIdType.MESH)

        repeat(1, size, greet)
    pl.semaphore_wait(barrier, count)

    def remote(src, dst, send, recv, target):
        return pltpu.make_async_remote_copy(
            src_ref=src,
            dst_ref=dst,
            send_sem=send,
            recv_sem=recv,
            device_id={"psg": target},
            device_id_type=pl.DeviceIdType.MESH,
        )

    if gathered:
        j, z = lax.rem(me, slices), me // slices
        parity = lax.rem(j, 2)
        partner = me + 1 - 2 * parity
        layers = devices // slices
        mine, pair = sources[n], outs[n]
        send, recv, pair_send, pair_recv, own = sems[3 * n :]
        along = []
        for r in range(1, layers):
            target = lax.rem(z + r, layers) * slices + j
            along.append(remote(mine, pair.at[parity, z], send.at[r], recv.at[r], target))
            along[-1].start()
        across = [remote(mine, pair.at[parity, z], pair_send.at[0], pair_recv.at[0], partner)]
        across[0].start()
        kept = pltpu.make_async_copy(mine, pair.at[parity, z], own)
        kept.start()

    moves, stays = [], []
    for i, kind in enumerate(kinds):
        size, step = routes(kind, devices, slices, me)

        def copy(r, i=i, step=step):
            target, chunk, slot = step(r)
            return remote(
                sources[i].at[chunk], outs[i].at[slot], sems[3 * i].at[r], sems[3 * i + 1].at[r], target
            )

        moves.append((size, copy))
        chunk, slot = step(0)[1:]
        stays.append(pltpu.make_async_copy(sources[i].at[chunk], outs[i].at[slot], sems[3 * i + 2]))
    for size, copy in moves:
        repeat(1, size, lambda r, copy=copy: copy(r).start())
    for stay in stays:
        stay.start()

    if gathered:
        for r in range(1, layers):
            along[r - 1].wait_recv()
            landed = pair.at[parity, lax.rem(z - r + layers, layers)]
            across.append(remote(landed, landed, pair_send.at[r], pair_recv.at[r], partner))
            across[-1].start()
        for copy in along:
            copy.wait_send()
        for copy in across:
            copy.wait()
        kept.wait()
    for stay in stays:
        stay.wait()
    for size, copy in moves:
        repeat(1, size, lambda r, copy=copy: copy(r).wait())


def exchange(name, number, devices, slices, parts, gather=None):
    kinds = tuple(kind for kind, _ in parts)
    arrays = [array for _, array in parts]
    layers = devices // slices
    sizes = {"all": devices, "cast": devices, "layer": slices, "z": layers, "parity": slices // 2}
    shapes = [
        jax.ShapeDtypeStruct((sizes[kind],) + array.shape[1:], array.dtype) for kind, array in parts
    ]
    scratch = []
    for kind in kinds:
        scratch += [pltpu.SemaphoreType.DMA((sizes[kind],))] * 2 + [pltpu.SemaphoreType.DMA]
    if gather is not None:
        arrays.append(gather)
        shapes.append(jax.ShapeDtypeStruct((2, layers) + gather.shape, gather.dtype))
        scratch += [pltpu.SemaphoreType.DMA((layers,))] * 4 + [pltpu.SemaphoreType.DMA]
    anywhere = pl.BlockSpec(memory_space=pl.ANY)
    return pl.pallas_call(
        functools.partial(exchange_kernel, kinds, devices, slices, int(gather is not None)),
        out_shape=tuple(shapes),
        in_specs=[anywhere] * len(arrays),
        out_specs=tuple([anywhere] * len(shapes)),
        scratch_shapes=scratch,
        compiler_params=pltpu.CompilerParams(collective_id=number, has_side_effects=True),
        cost_estimate=pl.CostEstimate(flops=0, bytes_accessed=60 * 2**20, transcendentals=0),
        name=name,
    )(*arrays)


def send_to(src, dst, send, recv, target):
    return pltpu.make_async_remote_copy(
        src_ref=src,
        dst_ref=dst,
        send_sem=send,
        recv_sem=recv,
        device_id={"psg": target},
        device_id_type=pl.DeviceIdType.MESH,
    )


def inward_kernel(devices, slices, *refs):
    q_ref, g_ref, ld_ref, k_ref, v_ref, qg_out, ld_out, kv_out = refs[:8]
    in_send, in_recv, kv_send, kv_recv, ld_send, ld_recv, up_send, up_recv, down_send, down_recv, own = refs[8:]
    layers = devices // slices
    me = lax.axis_index("psg")
    j, z = lax.rem(me, slices), me // slices
    base = me - j
    lanes, width = q_ref.shape[1] // slices, k_ref.shape[1] // slices
    barrier = pltpu.get_barrier_semaphore()

    def greet(r, c):
        other = lax.rem(me + r, devices)
        pl.semaphore_signal(barrier, inc=1, device_id={"psg": other}, device_id_type=pl.DeviceIdType.MESH)
        return c

    lax.fori_loop(1, devices, greet, 0)
    pl.semaphore_wait(barrier, devices - 1)

    def columns(ref, part, size):
        return ref.at[:, pl.ds(pl.multiple_of(part * size, size), size)]

    def inside(r):
        other = lax.rem(j + r, slices)
        return [
            send_to(columns(ref, other, lanes), qg_out.at[me, i], in_send.at[i, r], in_recv.at[i, r], base + other)
            for i, ref in enumerate((q_ref, g_ref))
        ]

    def passages(r):
        other = lax.rem(j + r, slices)
        return [
            send_to(columns(ref, other, width), kv_out.at[j, i], kv_send.at[i, r], kv_recv.at[i, r], base + other)
            for i, ref in enumerate((k_ref, v_ref))
        ]

    def small(r):
        other = lax.rem(me + r, devices)
        return send_to(ld_ref.at[lax.rem(other, slices)], ld_out.at[me], ld_send.at[r], ld_recv.at[r], other)

    def hop(sent, r, up):
        layer = z - sent if up else z + sent
        source = layer * slices + lax.rem(j - r + slices, slices)
        ref = qg_out.at[source]
        if up:
            return send_to(ref, ref, up_send.at[sent, r], up_recv.at[sent, r], me + slices)
        return send_to(ref, ref, down_send.at[sent, r], down_recv.at[sent, r], me - slices)

    def hop_here(sent, r, up):
        layer = z - sent - 1 if up else z + sent + 1
        source = layer * slices + lax.rem(j - r + slices, slices)
        ref = qg_out.at[source]
        if up:
            return send_to(ref, ref, up_send.at[sent, r], up_recv.at[sent, r], lax.rem(me + 1, devices))
        return send_to(ref, ref, down_send.at[sent, r], down_recv.at[sent, r], lax.rem(me + 1, devices))

    kept = [
        pltpu.make_async_copy(columns(q_ref, j, lanes), qg_out.at[me, 0], own.at[0]),
        pltpu.make_async_copy(columns(g_ref, j, lanes), qg_out.at[me, 1], own.at[1]),
        pltpu.make_async_copy(columns(k_ref, j, width), kv_out.at[j, 0], own.at[2]),
        pltpu.make_async_copy(columns(v_ref, j, width), kv_out.at[j, 1], own.at[3]),
        pltpu.make_async_copy(ld_ref.at[j], ld_out.at[me], own.at[4]),
    ]
    for copy in kept:
        copy.start()
    for r in range(1, slices):
        for copy in inside(r):
            copy.start()
    for r in range(1, slices):
        for copy in passages(r):
            copy.start()
    for copy in kept:
        copy.wait()

    def forward(sent, r):
        @pl.when((z < layers - 1) & (z >= sent))
        def _():
            hop(sent, r, True).start()

        @pl.when((z > 0) & (z + sent < layers))
        def _():
            hop(sent, r, False).start()

    forward(0, 0)

    def first(r, c):
        for copy in inside(r):
            copy.wait_recv()
        forward(0, r)
        return c

    lax.fori_loop(1, slices, first, 0)
    lax.fori_loop(1, devices, lambda r, c: (small(r).start(), c)[1], 0)

    def later(n, c):
        sent, r = n // slices, lax.rem(n, slices)

        @pl.when(z > sent)
        def _():
            hop_here(sent, r, True).wait_recv()

        @pl.when((z > sent) & (z < layers - 1))
        def _():
            hop(sent + 1, r, True).start()

        @pl.when(z + sent + 1 < layers)
        def _():
            hop_here(sent, r, False).wait_recv()

        @pl.when((z + sent + 1 < layers) & (z > 0))
        def _():
            hop(sent + 1, r, False).start()

        return c

    lax.fori_loop(0, (layers - 1) * slices, later, 0)

    for r in range(1, slices):
        for copy in inside(r):
            copy.wait_send()
        for copy in passages(r):
            copy.wait()
    lax.fori_loop(1, devices, lambda r, c: (small(r).wait(), c)[1], 0)

    def ended(n, c):
        sent, r = n // slices, lax.rem(n, slices)

        @pl.when((z < layers - 1) & (z >= sent))
        def _():
            hop(sent, r, True).wait_send()

        @pl.when((z > 0) & (z + sent < layers))
        def _():
            hop(sent, r, False).wait_send()

        return c

    lax.fori_loop(0, (layers - 1) * slices, ended, 0)


def inward(devices, slices, queries, grad_out, ld, keys, values):
    layers = devices // slices
    row_count, columns = queries.shape
    span = keys.shape[0]
    dma = pltpu.SemaphoreType.DMA
    anywhere = pl.BlockSpec(memory_space=pl.ANY)
    return pl.pallas_call(
        functools.partial(inward_kernel, devices, slices),
        out_shape=(
            jax.ShapeDtypeStruct((devices, 2, row_count, columns // slices), queries.dtype),
            jax.ShapeDtypeStruct((devices,) + ld.shape[1:], ld.dtype),
            jax.ShapeDtypeStruct((slices, 2, span, keys.shape[1] // slices), keys.dtype),
        ),
        in_specs=[anywhere] * 5,
        out_specs=(anywhere,) * 3,
        scratch_shapes=[dma((2, slices))] * 4
        + [dma((devices,))] * 2
        + [dma((layers, slices))] * 4
        + [dma((5,))],
        compiler_params=pltpu.CompilerParams(collective_id=0, has_side_effects=True),
        cost_estimate=pl.CostEstimate(flops=0, bytes_accessed=60 * 2**20, transcendentals=0),
        name="exchange_in",
    )(queries, grad_out, ld, keys, values)


def outward_kernel(devices, slices, dq_ref, dkv_ref, w_ref, gq_out, dkv_out, hid_out, *scratch):
    terms, summed, pair, weight, hidden = scratch[:5]
    term_send, term_recv, up_send, up_recv, down_send, down_recv, pair_send, pair_recv = scratch[5:13]
    w_send, w_recv, dkv_send, dkv_recv, gq_send, gq_recv, hid_send, hid_recv, own = scratch[13:]
    layers = devices // slices
    quads = slices // 2
    me = lax.axis_index("psg")
    j, z = lax.rem(me, slices), me // slices
    base = me - j
    parity = lax.rem(j, 2)
    partner = me + 1 - 2 * parity
    row_count, lanes = dq_ref.shape[2:]
    chunk_rows = 2 * row_count
    barrier = pltpu.get_barrier_semaphore()

    def greet(r, c):
        other = lax.rem(me + r, devices)
        pl.semaphore_signal(barrier, inc=1, device_id={"psg": other}, device_id_type=pl.DeviceIdType.MESH)
        return c

    lax.fori_loop(1, devices, greet, 0)
    pl.semaphore_wait(barrier, devices - 1)

    def term(c, r, here=False):
        other = lax.rem(z + r, layers)
        slot = lax.rem(z - r + layers, layers) if here else z
        devs = slice(2 * c, 2 * c + 2)
        return send_to(
            dq_ref.at[other, devs], terms.at[slot, devs], term_send.at[c, r], term_recv.at[c, r],
            other * slices + j,
        )

    def weights(r):
        other = lax.rem(j // 2 + r, quads)
        width = 2 * lanes
        source = w_ref.at[:, pl.ds(pl.multiple_of(other * width, width), width)]
        if r == 0:
            return pltpu.make_async_copy(source, weight.at[j // 2], own.at[0])
        return send_to(
            source, weight.at[j // 2], w_send.at[r], w_recv.at[r], base + 2 * other + parity
        )

    def passages(r):
        other = lax.rem(j + r, slices)
        if r == 0:
            return pltpu.make_async_copy(dkv_ref.at[other], dkv_out.at[j], own.at[1])
        return send_to(dkv_ref.at[other], dkv_out.at[j], dkv_send.at[r], dkv_recv.at[r], base + other)

    def rows(r):
        other = lax.rem(j + r, slices)
        if r == 0:
            return pltpu.make_async_copy(summed.at[other], gq_out.at[j], own.at[2])
        return send_to(summed.at[other], gq_out.at[j], gq_send.at[r], gq_recv.at[r], base + other)

    def piece(core, layer, c):
        return pair.at[core, layer, c * chunk_rows : (c + 1) * chunk_rows]

    def hop(sent, c, up):
        ref = piece(parity, z - sent if up else z + sent, c)
        if up:
            return send_to(ref, ref, up_send.at[sent, c], up_recv.at[sent, c], me + slices)
        return send_to(ref, ref, down_send.at[sent, c], down_recv.at[sent, c], me - slices)

    def hop_here(sent, c, up):
        ref = piece(parity, z - sent - 1 if up else z + sent + 1, c)
        other = lax.rem(me + 1, devices)
        if up:
            return send_to(ref, ref, up_send.at[sent, c], up_recv.at[sent, c], other)
        return send_to(ref, ref, down_send.at[sent, c], down_recv.at[sent, c], other)

    def across(layer, c, here=False):
        ref = piece(1 - parity if here else parity, layer, c)
        return send_to(ref, ref, pair_send.at[layer, c], pair_recv.at[layer, c], partner)

    def columns(layer, r):
        other = lax.rem(j + r, slices)
        target = layer * slices + other
        step = lax.rem(target - me + devices, devices)
        return send_to(
            hidden.at[layer, other], hid_out.at[me], hid_send.at[step], hid_recv.at[step], target
        )

    def product(layer):
        for c in range(quads):
            across(layer, c, True).wait_recv()
        matrix = weight[...].reshape(-1, 2 * lanes)
        out = dot(pair[0, layer], matrix[:, :lanes], NT) + dot(pair[1, layer], matrix[:, lanes:], NT)
        hidden[layer] = out.astype(hidden.dtype).reshape(hidden.shape[1:])

    for c in range(quads):
        for r in range(1, layers):
            term(c, r).start()
    for r in range(quads):
        weights(r).start()
    for r in range(slices):
        passages(r).start()

    for c in range(quads):
        devs = slice(2 * c, 2 * c + 2)
        total = dq_ref[z, devs].astype(jnp.float32)
        for r in range(1, layers):
            term(c, r, True).wait_recv()
            total += terms[lax.rem(z - r + layers, layers), devs].astype(jnp.float32)
        summed[devs] = total
        pair[parity, z, c * chunk_rows : (c + 1) * chunk_rows] = total.astype(pair.dtype).reshape(
            chunk_rows, lanes
        )

        @pl.when(z < layers - 1)
        def _():
            hop(0, c, True).start()

        @pl.when(z > 0)
        def _():
            hop(0, c, False).start()

        across(z, c).start()

    for r in range(1, quads):
        weights(r).wait_recv()
    weights(0).wait()
    product(z)
    for r in range(1, slices):
        columns(z, r).start()
    kept = pltpu.make_async_copy(hidden.at[z, j], hid_out.at[me], own.at[3])
    kept.start()
    for r in range(slices):
        rows(r).start()

    for sent in range(layers - 1):
        for c in range(quads):

            @pl.when(z > sent)
            def _():
                hop_here(sent, c, True).wait_recv()
                across(z - sent - 1, c).start()

            @pl.when((z > sent) & (z < layers - 1))
            def _():
                hop(sent + 1, c, True).start()

            @pl.when(z + sent + 1 < layers)
            def _():
                hop_here(sent, c, False).wait_recv()
                across(z + sent + 1, c).start()

            @pl.when((z + sent + 1 < layers) & (z > 0))
            def _():
                hop(sent + 1, c, False).start()

        @pl.when(z > sent)
        def _():
            product(z - sent - 1)
            for r in range(slices):
                columns(z - sent - 1, r).start()

        @pl.when(z + sent + 1 < layers)
        def _():
            product(z + sent + 1)
            for r in range(slices):
                columns(z + sent + 1, r).start()

    for c in range(quads):
        for r in range(1, layers):
            term(c, r).wait_send()
        for layer in range(layers):
            across(layer, c).wait_send()
        for sent in range(layers - 1):

            @pl.when((z < layers - 1) & (z >= sent))
            def _():
                hop(sent, c, True).wait_send()

            @pl.when((z > 0) & (z + sent < layers))
            def _():
                hop(sent, c, False).wait_send()

    for r in range(1, quads):
        weights(r).wait_send()
    for r in range(slices):
        passages(r).wait()
        rows(r).wait()
    kept.wait()

    def arrived(r, c):
        target = lax.rem(me + r, devices)
        send_to(
            hidden.at[target // slices, lax.rem(target, slices)],
            hid_out.at[lax.rem(me - r + devices, devices)],
            hid_send.at[r],
            hid_recv.at[r],
            target,
        ).wait()
        return c

    lax.fori_loop(1, devices, arrived, 0)


def outward(devices, slices, dq, dkv, weight):
    layers, quads = devices // slices, slices // 2
    _, _, row_count, lanes = dq.shape
    out_columns = weight.shape[0]
    dma = pltpu.SemaphoreType.DMA
    anywhere = pl.BlockSpec(memory_space=pl.ANY)
    return pl.pallas_call(
        functools.partial(outward_kernel, devices, slices),
        out_shape=(
            jax.ShapeDtypeStruct((slices, row_count, lanes), jnp.float32),
            jax.ShapeDtypeStruct(dkv.shape, dkv.dtype),
            jax.ShapeDtypeStruct((devices, row_count, quads * out_columns), jnp.bfloat16),
        ),
        in_specs=[pl.BlockSpec(memory_space=pltpu.VMEM), anywhere, anywhere],
        out_specs=(anywhere,) * 3,
        scratch_shapes=[
            pltpu.VMEM(dq.shape, dq.dtype),
            pltpu.VMEM((slices, row_count, lanes), jnp.float32),
            pltpu.VMEM((2, layers, slices * row_count, lanes), jnp.bfloat16),
            pltpu.VMEM((quads, out_columns, 2 * lanes), weight.dtype),
            pltpu.VMEM((layers, slices, row_count, quads * out_columns), jnp.bfloat16),
        ]
        + [dma((quads, layers))] * 2
        + [dma((layers, quads))] * 6
        + [dma((quads,))] * 2
        + [dma((slices,))] * 4
        + [dma((devices,))] * 2
        + [dma((4,))],
        compiler_params=pltpu.CompilerParams(
            collective_id=1, has_side_effects=True, vmem_limit_bytes=40 * 2**20
        ),
        cost_estimate=pl.CostEstimate(flops=2 * 2**29, bytes_accessed=60 * 2**20, transcendentals=0),
        name="exchange_out",
    )(dq, dkv, weight)


def finish_kernel(slices, steps, dkv_ref, hidden_ref, gq_ref, dk_ref, dv_ref, out_ref, dq_ref):
    step = pl.program_id(0)
    quads = slices // 2
    layers, width = hidden_ref.shape[0], hidden_ref.shape[-1] // quads
    head, lanes = dkv_ref.shape[-1], gq_ref.shape[-1]
    for h in range(2):
        dk_ref[:, h * head : (h + 1) * head] = dkv_ref[h, 0].astype(jnp.float32)
        dv_ref[:, h * head : (h + 1) * head] = dkv_ref[h, 1].astype(jnp.float32)
    for z in range(layers):

        @pl.when(step == z % steps)
        def _():
            for parity in range(2):
                total = hidden_ref[z, 0, parity].astype(jnp.float32)
                for k in range(1, quads):
                    total += hidden_ref[z, k, parity].astype(jnp.float32)
                for k in range(quads):
                    first = (z * slices + 2 * k + parity) * width
                    out_ref[:, first : first + width] = total[:, k * width : (k + 1) * width]

    @pl.when(step == steps - 1)
    def _():
        for p in range(slices):
            dq_ref[:, p * lanes : (p + 1) * lanes] = gq_ref[p]


def finish(slices, dkv, hidden, summed):
    _, _, span, width = dkv.shape
    layers, quads, _, row_count, part = hidden.shape
    steps = slices // 2
    out = jax.ShapeDtypeStruct((span, slices * width), jnp.float32)
    whole = lambda shape: pl.BlockSpec(shape, lambda s: (0,) * len(shape))
    hidden_shape = (row_count, layers * 2 * part)
    query_shape = (row_count, slices * summed.shape[2])
    return pl.pallas_call(
        functools.partial(finish_kernel, slices, steps),
        out_shape=(
            out,
            out,
            jax.ShapeDtypeStruct(hidden_shape, jnp.float32),
            jax.ShapeDtypeStruct(query_shape, jnp.float32),
        ),
        grid=(steps,),
        in_specs=[
            pl.BlockSpec((2, 2, span, width), lambda s: (s, 0, 0, 0)),
            whole(hidden.shape),
            whole(summed.shape),
        ],
        out_specs=(
            pl.BlockSpec((span, 2 * width), lambda s: (0, s)),
            pl.BlockSpec((span, 2 * width), lambda s: (0, s)),
            whole(hidden_shape),
            whole(query_shape),
        ),
        compiler_params=pltpu.CompilerParams(vmem_limit_bytes=58 * 2**20),
        cost_estimate=pl.CostEstimate(flops=0, bytes_accessed=8 * 2**20, transcendentals=0),
        name="finish",
    )(dkv, hidden, summed)


def on_device(queries, grad_out, attn_out, log_sum, keys, values, proj_weight, attend, qlen):
    row_count, columns = queries.shape
    head_count = log_sum.shape[0]
    slices = head_count // GROUP
    span = keys.shape[0]
    devices = lax.axis_size("psg")
    layers = devices // slices
    me = lax.axis_index("psg")
    lanes = GROUP * ATTN_WIDTH
    wide = GROUP * row_count
    run = functools.partial(exchange, devices=devices, slices=slices)

    products = grad_out.astype(jnp.float32) * attn_out.astype(jnp.float32)
    delta = jnp.sum(products.reshape(row_count, head_count, ATTN_WIDTH), axis=2).T
    ld = jnp.stack([log_sum * LOG2_E, delta])
    ld = ld.reshape(2, slices, wide).transpose(1, 0, 2)
    if slices > 1:
        qg, ld, kv = inward(devices, slices, queries, grad_out, ld, keys, values)
    else:
        kv = jnp.stack([keys, values])[None]
        qg = jnp.stack([queries, grad_out])[None]
        qg, ld = run("exchange_in", 0, parts=[("cast", qg), ("cast", ld)])

    out_dtype = jnp.bfloat16 if slices > 1 else jnp.float32
    dkv, dq = attention(attend, qlen, kv, qg, ld, out_dtype)

    dq = dq.reshape(layers, slices, row_count, lanes)
    out_columns = proj_weight.shape[0]
    if slices > 1:
        summed, dkv, hidden = outward(devices, slices, dq, dkv, proj_weight)
        hidden = hidden.reshape(layers, slices // 2, 2, row_count, slices // 2 * out_columns)
        grad_keys, grad_values, hidden, grad_query = finish(slices, dkv, hidden, summed)
    else:
        (dq,) = run("exchange_terms", 1, parts=[("all", dq)])
        summed = jnp.sum(dq.astype(jnp.float32), axis=0)
        low = summed.astype(jnp.bfloat16).reshape(row_count, lanes)
        all_low = lax.all_gather(low, "psg", axis=0, tiled=True)
        hidden = dot(all_low, proj_weight, NT)
        hidden = lax.all_to_all(hidden.reshape(devices, row_count, out_columns), "psg", 0, 0)
        hidden = hidden.transpose(1, 0, 2).reshape(row_count, devices * out_columns)
        grad_keys, grad_values = dkv[0, 0], dkv[0, 1]
        grad_query = summed.reshape(row_count, columns)
    grad_hidden = lax.psum(hidden, "qry")
    return (grad_query, grad_keys, grad_values, grad_hidden)


def solution(mesh):
    in_specs = (
        P("psg", "qry"),
        P("psg", "qry"),
        P("psg", "qry"),
        P("qry", "psg"),
        P("psg", "qry"),
        P("psg", "qry"),
        P("psg", "qry"),
        P(),
        P(),
    )
    out_specs = (P("psg", "qry"), P("psg", "qry"), P("psg", "qry"), P("psg", None))
    return jax.shard_map(
        on_device, mesh=mesh, in_specs=in_specs, out_specs=out_specs, check_vma=False
    )
```

```python
import functools

import jax
import jax.numpy as jnp
from jax import lax
from jax.experimental import pallas as pl
from jax.experimental.pallas import tpu as pltpu
from jax.sharding import PartitionSpec as P

ATTN_WIDTH = 128
GROUP = 4
PADDED_ASK_LEN = 256
TILE = 128
LOG2_E = 1.4426950408889634
SCALE = ATTN_WIDTH ** (-0.5)
NT = (((1,), (1,)), ((), ()))
NN = (((1,), (0,)), ((), ()))


def dot(a, b, dims=NN):
    return lax.dot_general(a, b, dims, preferred_element_type=jnp.float32)


def head_rows(qg_ref, first, per_part, which):
    pieces = [
        qg_ref[first + k, which, :, h * ATTN_WIDTH : (h + 1) * ATTN_WIDTH]
        for k in range(per_part)
        for h in range(GROUP)
    ]
    return jnp.concatenate(pieces, axis=0)


def attention_kernel(
    blocks, tile_count, per_tile, attend, qlen, kv_ref, qg_ref, ld_ref, dkv_ref, dq_ref, dk_acc, dv_acc, dq_acc
):
    block = pl.program_id(0)
    per_part = per_tile // 2
    row_count = TILE // per_tile
    wide = GROUP * row_count

    @pl.when(block == 0)
    def _():
        dq_acc[...] = jnp.zeros_like(dq_acc)

    dk_acc[...] = jnp.zeros_like(dk_acc)
    dv_acc[...] = jnp.zeros_like(dv_acc)
    key_rows_t = kv_ref[0, 0].T

    def visit(first_tile, tile_total):
        keys, values = kv_ref[0, 0], kv_ref[0, 1]
        dk, dv = None, None
        for step in range(2 * tile_total):
            tile, part = first_tile + step // 2, step % 2
            rows = slice(part * 256, part * 256 + 256)
            first = tile * per_tile + part * per_part
            q = head_rows(qg_ref, first, per_part, 0)
            g = head_rows(qg_ref, first, per_part, 1)
            ld = jnp.concatenate([ld_ref[first + k] for k in range(per_part)], axis=1)
            lse, delta = ld[0:1], ld[1:2]
            prob = jnp.exp2(dot(keys, q, NT) * (SCALE * LOG2_E) - lse)
            dprob = dot(values, g, NT)
            dscore = (prob * (dprob - delta)).astype(jnp.bfloat16)
            v_term = dot(prob.astype(jnp.bfloat16), g)
            k_term = dot(dscore, q)
            dv = v_term if dv is None else dv + v_term
            dk = k_term if dk is None else dk + k_term
            dq_acc[tile, :, rows] += dot(key_rows_t, dscore)
        dk_acc[...] += dk
        dv_acc[...] += dv

    mine = lax.axis_index("psg")
    mine = mine - lax.rem(mine, blocks) + block
    questions, named = attend.shape

    def ask(question, carry):
        hits = attend[question, 0] == mine
        for i in range(1, named):
            hits = hits | (attend[question, i] == mine)
        most = PADDED_ASK_LEN // TILE
        for count in range(1, most + 1):

            @pl.when(hits & (qlen[question] // TILE == count))
            def _():
                visit(question * most, count)

        return carry

    lax.fori_loop(0, questions, ask, 0)
    dkv_ref[0, 0] = (dk_acc[...] * SCALE).astype(dkv_ref.dtype)
    dkv_ref[0, 1] = dv_acc[...].astype(dkv_ref.dtype)

    @pl.when(block == blocks - 1)
    def _():
        def put(tile, carry):
            for k in range(per_tile):
                piece = dq_acc[tile, :, k * wide : (k + 1) * wide] * SCALE
                piece = piece.T.astype(dq_ref.dtype)
                for h in range(GROUP):
                    cols = slice(h * ATTN_WIDTH, (h + 1) * ATTN_WIDTH)
                    dq_ref[tile * per_tile + k, :, cols] = piece[h * row_count : (h + 1) * row_count]
            return carry

        lax.fori_loop(0, tile_count, put, 0)


def attention(attend, qlen, kv, qg, ld, out_dtype):
    blocks, _, span, width = kv.shape
    sources, _, row_count, lanes = qg.shape
    per_tile = TILE // row_count
    tile_count = sources // per_tile
    whole = lambda shape: pl.BlockSpec(shape, lambda b, *_: (0,) * len(shape))
    return pl.pallas_call(
        functools.partial(attention_kernel, blocks, tile_count, per_tile),
        out_shape=(
            jax.ShapeDtypeStruct(kv.shape, out_dtype),
            jax.ShapeDtypeStruct((sources, row_count, lanes), jnp.bfloat16),
        ),
        grid_spec=pltpu.PrefetchScalarGridSpec(
            num_scalar_prefetch=2,
            grid=(blocks,),
            in_specs=[
                pl.BlockSpec((1, 2, span, width), lambda b, *_: (b, 0, 0, 0)),
                whole(qg.shape),
                whole(ld.shape),
            ],
            out_specs=(
                pl.BlockSpec((1, 2, span, width), lambda b, *_: (b, 0, 0, 0)),
                whole((sources, row_count, lanes)),
            ),
            scratch_shapes=[
                pltpu.VMEM((span, width), jnp.float32),
                pltpu.VMEM((span, width), jnp.float32),
                pltpu.VMEM((tile_count, width, lanes), jnp.float32),
            ],
        ),
        compiler_params=pltpu.CompilerParams(vmem_limit_bytes=58 * 2**20),
        cost_estimate=pl.CostEstimate(
            flops=2 * blocks * span * width * lanes * tile_count * 5 // 2,
            bytes_accessed=16 * 2**20,
            transcendentals=blocks * span * lanes * tile_count // 2,
        ),
        name="attention",
    )(attend, qlen, kv, qg, ld)


def routes(kind, devices, slices, me):
    layers = devices // slices
    j, z = lax.rem(me, slices), me // slices
    base = me - j
    if kind in ("all", "cast"):

        def step(r):
            target = lax.rem(me + r, devices)
            return target, (target if kind == "all" else lax.rem(target, slices)), me

        return devices, step
    if kind == "layer":

        def step(r):
            other = lax.rem(j + r, slices)
            return base + other, other, j

        return slices, step
    if kind == "z":

        def step(r):
            other = lax.rem(z + r, layers)
            return other * slices + j, other, z

        return layers, step
    quads = slices // 2

    def step(r):
        other = lax.rem(j // 2 + r, quads)
        return base + 2 * other + lax.rem(j, 2), other, j // 2

    return quads, step


def repeat(first, count, body):
    if count - first <= 8:
        for r in range(first, count):
            body(r)
    else:
        lax.fori_loop(first, count, lambda r, c: (body(r), c)[1], 0)


def exchange_kernel(kinds, devices, slices, gathered, *refs):
    n = len(kinds)
    total = n + gathered
    sources, outs = refs[:total], refs[total : 2 * total]
    sems = refs[2 * total :]
    me = lax.axis_index("psg")
    barrier = pltpu.get_barrier_semaphore()
    if "all" in kinds or "cast" in kinds:
        greeted = ("all",)
    else:
        greeted = ("z", "layer")
    count = 0
    for kind in greeted:
        size, step = routes(kind, devices, slices, me)
        count += size - 1

        def greet(r, step=step):
            pl.semaphore_signal(barrier, inc=1, device_id={"psg": step(r)[0]}, device_id_type=pl.DeviceIdType.MESH)

        repeat(1, size, greet)
    pl.semaphore_wait(barrier, count)

    def remote(src, dst, send, recv, target):
        return pltpu.make_async_remote_copy(
            src_ref=src,
            dst_ref=dst,
            send_sem=send,
            recv_sem=recv,
            device_id={"psg": target},
            device_id_type=pl.DeviceIdType.MESH,
        )

    if gathered:
        j, z = lax.rem(me, slices), me // slices
        parity = lax.rem(j, 2)
        partner = me + 1 - 2 * parity
        layers = devices // slices
        mine, pair = sources[n], outs[n]
        send, recv, pair_send, pair_recv, own = sems[3 * n :]
        along = []
        for r in range(1, layers):
            target = lax.rem(z + r, layers) * slices + j
            along.append(remote(mine, pair.at[parity, z], send.at[r], recv.at[r], target))
            along[-1].start()
        across = [remote(mine, pair.at[parity, z], pair_send.at[0], pair_recv.at[0], partner)]
        across[0].start()
        kept = pltpu.make_async_copy(mine, pair.at[parity, z], own)
        kept.start()

    moves, stays = [], []
    for i, kind in enumerate(kinds):
        size, step = routes(kind, devices, slices, me)

        def copy(r, i=i, step=step):
            target, chunk, slot = step(r)
            return remote(
                sources[i].at[chunk], outs[i].at[slot], sems[3 * i].at[r], sems[3 * i + 1].at[r], target
            )

        moves.append((size, copy))
        chunk, slot = step(0)[1:]
        stays.append(pltpu.make_async_copy(sources[i].at[chunk], outs[i].at[slot], sems[3 * i + 2]))
    for size, copy in moves:
        repeat(1, size, lambda r, copy=copy: copy(r).start())
    for stay in stays:
        stay.start()

    if gathered:
        for r in range(1, layers):
            along[r - 1].wait_recv()
            landed = pair.at[parity, lax.rem(z - r + layers, layers)]
            across.append(remote(landed, landed, pair_send.at[r], pair_recv.at[r], partner))
            across[-1].start()
        for copy in along:
            copy.wait_send()
        for copy in across:
            copy.wait()
        kept.wait()
    for stay in stays:
        stay.wait()
    for size, copy in moves:
        repeat(1, size, lambda r, copy=copy: copy(r).wait())


def exchange(name, number, devices, slices, parts, gather=None):
    kinds = tuple(kind for kind, _ in parts)
    arrays = [array for _, array in parts]
    layers = devices // slices
    sizes = {"all": devices, "cast": devices, "layer": slices, "z": layers, "parity": slices // 2}
    shapes = [
        jax.ShapeDtypeStruct((sizes[kind],) + array.shape[1:], array.dtype) for kind, array in parts
    ]
    scratch = []
    for kind in kinds:
        scratch += [pltpu.SemaphoreType.DMA((sizes[kind],))] * 2 + [pltpu.SemaphoreType.DMA]
    if gather is not None:
        arrays.append(gather)
        shapes.append(jax.ShapeDtypeStruct((2, layers) + gather.shape, gather.dtype))
        scratch += [pltpu.SemaphoreType.DMA((layers,))] * 4 + [pltpu.SemaphoreType.DMA]
    anywhere = pl.BlockSpec(memory_space=pl.ANY)
    return pl.pallas_call(
        functools.partial(exchange_kernel, kinds, devices, slices, int(gather is not None)),
        out_shape=tuple(shapes),
        in_specs=[anywhere] * len(arrays),
        out_specs=tuple([anywhere] * len(shapes)),
        scratch_shapes=scratch,
        compiler_params=pltpu.CompilerParams(collective_id=number, has_side_effects=True),
        cost_estimate=pl.CostEstimate(flops=0, bytes_accessed=60 * 2**20, transcendentals=0),
        name=name,
    )(*arrays)


def send_to(src, dst, send, recv, target):
    return pltpu.make_async_remote_copy(
        src_ref=src,
        dst_ref=dst,
        send_sem=send,
        recv_sem=recv,
        device_id={"psg": target},
        device_id_type=pl.DeviceIdType.MESH,
    )


def inward_kernel(devices, slices, *refs):
    q_ref, g_ref, ld_ref, k_ref, v_ref, qg_out, ld_out, kv_out = refs[:8]
    in_send, in_recv, kv_send, kv_recv, ld_send, ld_recv, up_send, up_recv, down_send, down_recv, own = refs[8:]
    layers = devices // slices
    me = lax.axis_index("psg")
    j, z = lax.rem(me, slices), me // slices
    base = me - j
    lanes, width = q_ref.shape[1] // slices, k_ref.shape[1] // slices
    barrier = pltpu.get_barrier_semaphore()

    def greet(r, c):
        other = lax.rem(me + r, devices)
        pl.semaphore_signal(barrier, inc=1, device_id={"psg": other}, device_id_type=pl.DeviceIdType.MESH)
        return c

    lax.fori_loop(1, devices, greet, 0)
    pl.semaphore_wait(barrier, devices - 1)

    def columns(ref, part, size):
        return ref.at[:, pl.ds(pl.multiple_of(part * size, size), size)]

    def inside(r):
        other = lax.rem(j + r, slices)
        return [
            send_to(columns(ref, other, lanes), qg_out.at[me, i], in_send.at[i, r], in_recv.at[i, r], base + other)
            for i, ref in enumerate((q_ref, g_ref))
        ]

    def passages(r):
        other = lax.rem(j + r, slices)
        return [
            send_to(columns(ref, other, width), kv_out.at[j, i], kv_send.at[i, r], kv_recv.at[i, r], base + other)
            for i, ref in enumerate((k_ref, v_ref))
        ]

    def small(r):
        other = lax.rem(me + r, devices)
        return send_to(ld_ref.at[lax.rem(other, slices)], ld_out.at[me], ld_send.at[r], ld_recv.at[r], other)

    def hop(sent, r, up):
        layer = z - sent if up else z + sent
        source = layer * slices + lax.rem(j - r + slices, slices)
        ref = qg_out.at[source]
        if up:
            return send_to(ref, ref, up_send.at[sent, r], up_recv.at[sent, r], me + slices)
        return send_to(ref, ref, down_send.at[sent, r], down_recv.at[sent, r], me - slices)

    def hop_here(sent, r, up):
        layer = z - sent - 1 if up else z + sent + 1
        source = layer * slices + lax.rem(j - r + slices, slices)
        ref = qg_out.at[source]
        if up:
            return send_to(ref, ref, up_send.at[sent, r], up_recv.at[sent, r], lax.rem(me + 1, devices))
        return send_to(ref, ref, down_send.at[sent, r], down_recv.at[sent, r], lax.rem(me + 1, devices))

    kept = [
        pltpu.make_async_copy(columns(q_ref, j, lanes), qg_out.at[me, 0], own.at[0]),
        pltpu.make_async_copy(columns(g_ref, j, lanes), qg_out.at[me, 1], own.at[1]),
        pltpu.make_async_copy(columns(k_ref, j, width), kv_out.at[j, 0], own.at[2]),
        pltpu.make_async_copy(columns(v_ref, j, width), kv_out.at[j, 1], own.at[3]),
        pltpu.make_async_copy(ld_ref.at[j], ld_out.at[me], own.at[4]),
    ]
    for copy in kept:
        copy.start()
    for r in range(1, slices):
        for copy in inside(r):
            copy.start()
    for r in range(1, slices):
        for copy in passages(r):
            copy.start()
    for copy in kept:
        copy.wait()

    def forward(sent, r):
        @pl.when((z < layers - 1) & (z >= sent))
        def _():
            hop(sent, r, True).start()

        @pl.when((z > 0) & (z + sent < layers))
        def _():
            hop(sent, r, False).start()

    forward(0, 0)

    def first(r, c):
        for copy in inside(r):
            copy.wait_recv()
        forward(0, r)
        return c

    lax.fori_loop(1, slices, first, 0)
    lax.fori_loop(1, devices, lambda r, c: (small(r).start(), c)[1], 0)

    def later(n, c):
        sent, r = n // slices, lax.rem(n, slices)

        @pl.when(z > sent)
        def _():
            hop_here(sent, r, True).wait_recv()

        @pl.when((z > sent) & (z < layers - 1))
        def _():
            hop(sent + 1, r, True).start()

        @pl.when(z + sent + 1 < layers)
        def _():
            hop_here(sent, r, False).wait_recv()

        @pl.when((z + sent + 1 < layers) & (z > 0))
        def _():
            hop(sent + 1, r, False).start()

        return c

    lax.fori_loop(0, (layers - 1) * slices, later, 0)

    for r in range(1, slices):
        for copy in inside(r):
            copy.wait_send()
        for copy in passages(r):
            copy.wait()
    lax.fori_loop(1, devices, lambda r, c: (small(r).wait(), c)[1], 0)

    def ended(n, c):
        sent, r = n // slices, lax.rem(n, slices)

        @pl.when((z < layers - 1) & (z >= sent))
        def _():
            hop(sent, r, True).wait_send()

        @pl.when((z > 0) & (z + sent < layers))
        def _():
            hop(sent, r, False).wait_send()

        return c

    lax.fori_loop(0, (layers - 1) * slices, ended, 0)


def inward(devices, slices, queries, grad_out, ld, keys, values):
    layers = devices // slices
    row_count, columns = queries.shape
    span = keys.shape[0]
    dma = pltpu.SemaphoreType.DMA
    anywhere = pl.BlockSpec(memory_space=pl.ANY)
    return pl.pallas_call(
        functools.partial(inward_kernel, devices, slices),
        out_shape=(
            jax.ShapeDtypeStruct((devices, 2, row_count, columns // slices), queries.dtype),
            jax.ShapeDtypeStruct((devices,) + ld.shape[1:], ld.dtype),
            jax.ShapeDtypeStruct((slices, 2, span, keys.shape[1] // slices), keys.dtype),
        ),
        in_specs=[anywhere] * 5,
        out_specs=(anywhere,) * 3,
        scratch_shapes=[dma((2, slices))] * 4
        + [dma((devices,))] * 2
        + [dma((layers, slices))] * 4
        + [dma((5,))],
        compiler_params=pltpu.CompilerParams(collective_id=0, has_side_effects=True),
        cost_estimate=pl.CostEstimate(flops=0, bytes_accessed=60 * 2**20, transcendentals=0),
        name="exchange_in",
    )(queries, grad_out, ld, keys, values)


def outward_kernel(devices, slices, dq_ref, dkv_ref, w_ref, gq_out, dkv_out, hid_out, *scratch):
    terms, summed, pair, weight, hidden = scratch[:5]
    term_send, term_recv, up_send, up_recv, down_send, down_recv, pair_send, pair_recv = scratch[5:13]
    w_send, w_recv, dkv_send, dkv_recv, gq_send, gq_recv, hid_send, hid_recv, own = scratch[13:]
    layers = devices // slices
    quads = slices // 2
    me = lax.axis_index("psg")
    j, z = lax.rem(me, slices), me // slices
    base = me - j
    parity = lax.rem(j, 2)
    partner = me + 1 - 2 * parity
    row_count, lanes = dq_ref.shape[2:]
    chunk_rows = 2 * row_count
    barrier = pltpu.get_barrier_semaphore()

    def greet(r, c):
        other = lax.rem(me + r, devices)
        pl.semaphore_signal(barrier, inc=1, device_id={"psg": other}, device_id_type=pl.DeviceIdType.MESH)
        return c

    lax.fori_loop(1, devices, greet, 0)
    pl.semaphore_wait(barrier, devices - 1)

    def term(c, r, here=False):
        other = lax.rem(z + r, layers)
        slot = lax.rem(z - r + layers, layers) if here else z
        devs = slice(2 * c, 2 * c + 2)
        return send_to(
            dq_ref.at[other, devs], terms.at[slot, devs], term_send.at[c, r], term_recv.at[c, r],
            other * slices + j,
        )

    def weights(r):
        other = lax.rem(j // 2 + r, quads)
        width = 2 * lanes
        source = w_ref.at[:, pl.ds(pl.multiple_of(other * width, width), width)]
        if r == 0:
            return pltpu.make_async_copy(source, weight.at[j // 2], own.at[0])
        return send_to(
            source, weight.at[j // 2], w_send.at[r], w_recv.at[r], base + 2 * other + parity
        )

    def passages(r):
        other = lax.rem(j + r, slices)
        if r == 0:
            return pltpu.make_async_copy(dkv_ref.at[other], dkv_out.at[j], own.at[1])
        return send_to(dkv_ref.at[other], dkv_out.at[j], dkv_send.at[r], dkv_recv.at[r], base + other)

    def rows(r):
        other = lax.rem(j + r, slices)
        if r == 0:
            return pltpu.make_async_copy(summed.at[other], gq_out.at[j], own.at[2])
        return send_to(summed.at[other], gq_out.at[j], gq_send.at[r], gq_recv.at[r], base + other)

    def piece(core, layer, c):
        return pair.at[core, layer, c * chunk_rows : (c + 1) * chunk_rows]

    def hop(sent, c, up):
        ref = piece(parity, z - sent if up else z + sent, c)
        if up:
            return send_to(ref, ref, up_send.at[sent, c], up_recv.at[sent, c], me + slices)
        return send_to(ref, ref, down_send.at[sent, c], down_recv.at[sent, c], me - slices)

    def hop_here(sent, c, up):
        ref = piece(parity, z - sent - 1 if up else z + sent + 1, c)
        other = lax.rem(me + 1, devices)
        if up:
            return send_to(ref, ref, up_send.at[sent, c], up_recv.at[sent, c], other)
        return send_to(ref, ref, down_send.at[sent, c], down_recv.at[sent, c], other)

    def across(layer, c, here=False):
        ref = piece(1 - parity if here else parity, layer, c)
        return send_to(ref, ref, pair_send.at[layer, c], pair_recv.at[layer, c], partner)

    def columns(layer, r):
        other = lax.rem(j + r, slices)
        target = layer * slices + other
        step = lax.rem(target - me + devices, devices)
        return send_to(
            hidden.at[layer, other], hid_out.at[me], hid_send.at[step], hid_recv.at[step], target
        )

    def product(layer):
        for c in range(quads):
            across(layer, c, True).wait_recv()
        matrix = weight[...].reshape(-1, 2 * lanes)
        out = dot(pair[0, layer], matrix[:, :lanes], NT) + dot(pair[1, layer], matrix[:, lanes:], NT)
        hidden[layer] = out.astype(hidden.dtype).reshape(hidden.shape[1:])

    for c in range(quads):
        for r in range(1, layers):
            term(c, r).start()
    for r in range(quads):
        weights(r).start()
    for r in range(slices):
        passages(r).start()

    for c in range(quads):
        devs = slice(2 * c, 2 * c + 2)
        total = dq_ref[z, devs].astype(jnp.float32)
        for r in range(1, layers):
            term(c, r, True).wait_recv()
            total += terms[lax.rem(z - r + layers, layers), devs].astype(jnp.float32)
        summed[devs] = total
        pair[parity, z, c * chunk_rows : (c + 1) * chunk_rows] = total.astype(pair.dtype).reshape(
            chunk_rows, lanes
        )

        @pl.when(z < layers - 1)
        def _():
            hop(0, c, True).start()

        @pl.when(z > 0)
        def _():
            hop(0, c, False).start()

        across(z, c).start()

    for r in range(1, quads):
        weights(r).wait_recv()
    weights(0).wait()
    product(z)
    for r in range(1, slices):
        columns(z, r).start()
    kept = pltpu.make_async_copy(hidden.at[z, j], hid_out.at[me], own.at[3])
    kept.start()
    for r in range(slices):
        rows(r).start()

    for sent in range(layers - 1):
        for c in range(quads):

            @pl.when(z > sent)
            def _():
                hop_here(sent, c, True).wait_recv()
                across(z - sent - 1, c).start()

            @pl.when((z > sent) & (z < layers - 1))
            def _():
                hop(sent + 1, c, True).start()

            @pl.when(z + sent + 1 < layers)
            def _():
                hop_here(sent, c, False).wait_recv()
                across(z + sent + 1, c).start()

            @pl.when((z + sent + 1 < layers) & (z > 0))
            def _():
                hop(sent + 1, c, False).start()

        @pl.when(z > sent)
        def _():
            product(z - sent - 1)
            for r in range(slices):
                columns(z - sent - 1, r).start()

        @pl.when(z + sent + 1 < layers)
        def _():
            product(z + sent + 1)
            for r in range(slices):
                columns(z + sent + 1, r).start()

    for c in range(quads):
        for r in range(1, layers):
            term(c, r).wait_send()
        for layer in range(layers):
            across(layer, c).wait_send()
        for sent in range(layers - 1):

            @pl.when((z < layers - 1) & (z >= sent))
            def _():
                hop(sent, c, True).wait_send()

            @pl.when((z > 0) & (z + sent < layers))
            def _():
                hop(sent, c, False).wait_send()

    for r in range(1, quads):
        weights(r).wait_send()
    for r in range(slices):
        passages(r).wait()
        rows(r).wait()
    kept.wait()

    def arrived(r, c):
        target = lax.rem(me + r, devices)
        send_to(
            hidden.at[target // slices, lax.rem(target, slices)],
            hid_out.at[lax.rem(me - r + devices, devices)],
            hid_send.at[r],
            hid_recv.at[r],
            target,
        ).wait()
        return c

    lax.fori_loop(1, devices, arrived, 0)


def outward(devices, slices, dq, dkv, weight):
    layers, quads = devices // slices, slices // 2
    _, _, row_count, lanes = dq.shape
    out_columns = weight.shape[0]
    dma = pltpu.SemaphoreType.DMA
    anywhere = pl.BlockSpec(memory_space=pl.ANY)
    return pl.pallas_call(
        functools.partial(outward_kernel, devices, slices),
        out_shape=(
            jax.ShapeDtypeStruct((slices, row_count, lanes), jnp.float32),
            jax.ShapeDtypeStruct(dkv.shape, dkv.dtype),
            jax.ShapeDtypeStruct((devices, row_count, quads * out_columns), jnp.bfloat16),
        ),
        in_specs=[pl.BlockSpec(memory_space=pltpu.VMEM), anywhere, anywhere],
        out_specs=(anywhere,) * 3,
        scratch_shapes=[
            pltpu.VMEM(dq.shape, dq.dtype),
            pltpu.VMEM((slices, row_count, lanes), jnp.float32),
            pltpu.VMEM((2, layers, slices * row_count, lanes), jnp.bfloat16),
            pltpu.VMEM((quads, out_columns, 2 * lanes), weight.dtype),
            pltpu.VMEM((layers, slices, row_count, quads * out_columns), jnp.bfloat16),
        ]
        + [dma((quads, layers))] * 2
        + [dma((layers, quads))] * 6
        + [dma((quads,))] * 2
        + [dma((slices,))] * 4
        + [dma((devices,))] * 2
        + [dma((4,))],
        compiler_params=pltpu.CompilerParams(
            collective_id=1, has_side_effects=True, vmem_limit_bytes=58 * 2**20
        ),
        cost_estimate=pl.CostEstimate(flops=2 * 2**29, bytes_accessed=60 * 2**20, transcendentals=0),
        name="exchange_out",
    )(dq, dkv, weight)


def finish_kernel(slices, steps, dkv_ref, hidden_ref, gq_ref, dk_ref, dv_ref, out_ref, dq_ref):
    step = pl.program_id(0)
    quads = slices // 2
    layers, width = hidden_ref.shape[0], hidden_ref.shape[-1] // quads
    head, lanes = dkv_ref.shape[-1], gq_ref.shape[-1]
    for h in range(2):
        dk_ref[:, h * head : (h + 1) * head] = dkv_ref[h, 0].astype(jnp.float32)
        dv_ref[:, h * head : (h + 1) * head] = dkv_ref[h, 1].astype(jnp.float32)
    for z in range(layers):

        @pl.when(step == z % steps)
        def _():
            for parity in range(2):
                total = hidden_ref[z, 0, parity].astype(jnp.float32)
                for k in range(1, quads):
                    total += hidden_ref[z, k, parity].astype(jnp.float32)
                for k in range(quads):
                    first = (z * slices + 2 * k + parity) * width
                    out_ref[:, first : first + width] = total[:, k * width : (k + 1) * width]

    @pl.when(step == steps - 1)
    def _():
        for p in range(slices):
            dq_ref[:, p * lanes : (p + 1) * lanes] = gq_ref[p]


def finish(slices, dkv, hidden, summed):
    _, _, span, width = dkv.shape
    layers, quads, _, row_count, part = hidden.shape
    steps = slices // 2
    out = jax.ShapeDtypeStruct((span, slices * width), jnp.float32)
    whole = lambda shape: pl.BlockSpec(shape, lambda s: (0,) * len(shape))
    hidden_shape = (row_count, layers * 2 * part)
    query_shape = (row_count, slices * summed.shape[2])
    return pl.pallas_call(
        functools.partial(finish_kernel, slices, steps),
        out_shape=(
            out,
            out,
            jax.ShapeDtypeStruct(hidden_shape, jnp.float32),
            jax.ShapeDtypeStruct(query_shape, jnp.float32),
        ),
        grid=(steps,),
        in_specs=[
            pl.BlockSpec((2, 2, span, width), lambda s: (s, 0, 0, 0)),
            whole(hidden.shape),
            whole(summed.shape),
        ],
        out_specs=(
            pl.BlockSpec((span, 2 * width), lambda s: (0, s)),
            pl.BlockSpec((span, 2 * width), lambda s: (0, s)),
            whole(hidden_shape),
            whole(query_shape),
        ),
        compiler_params=pltpu.CompilerParams(vmem_limit_bytes=58 * 2**20),
        cost_estimate=pl.CostEstimate(flops=0, bytes_accessed=8 * 2**20, transcendentals=0),
        name="finish",
    )(dkv, hidden, summed)


def on_device(queries, grad_out, attn_out, log_sum, keys, values, proj_weight, attend, qlen):
    row_count, columns = queries.shape
    head_count = log_sum.shape[0]
    slices = head_count // GROUP
    span = keys.shape[0]
    devices = lax.axis_size("psg")
    layers = devices // slices
    me = lax.axis_index("psg")
    lanes = GROUP * ATTN_WIDTH
    wide = GROUP * row_count
    run = functools.partial(exchange, devices=devices, slices=slices)

    products = grad_out.astype(jnp.float32) * attn_out.astype(jnp.float32)
    delta = jnp.sum(products.reshape(row_count, head_count, ATTN_WIDTH), axis=2).T
    ld = jnp.stack([log_sum * LOG2_E, delta])
    ld = ld.reshape(2, slices, wide).transpose(1, 0, 2)
    if slices > 1:
        qg, ld, kv = inward(devices, slices, queries, grad_out, ld, keys, values)
    else:
        kv = jnp.stack([keys, values])[None]
        qg = jnp.stack([queries, grad_out])[None]
        qg, ld = run("exchange_in", 0, parts=[("cast", qg), ("cast", ld)])

    out_dtype = jnp.bfloat16 if slices > 1 else jnp.float32
    dkv, dq = attention(attend, qlen, kv, qg, ld, out_dtype)

    dq = dq.reshape(layers, slices, row_count, lanes)
    out_columns = proj_weight.shape[0]
    if slices > 1:
        summed, dkv, hidden = outward(devices, slices, dq, dkv, proj_weight)
        hidden = hidden.reshape(layers, slices // 2, 2, row_count, slices // 2 * out_columns)
        grad_keys, grad_values, hidden, grad_query = finish(slices, dkv, hidden, summed)
    else:
        (dq,) = run("exchange_terms", 1, parts=[("all", dq)])
        summed = jnp.sum(dq.astype(jnp.float32), axis=0)
        low = summed.astype(jnp.bfloat16).reshape(row_count, lanes)
        all_low = lax.all_gather(low, "psg", axis=0, tiled=True)
        hidden = dot(all_low, proj_weight, NT)
        hidden = lax.all_to_all(hidden.reshape(devices, row_count, out_columns), "psg", 0, 0)
        hidden = hidden.transpose(1, 0, 2).reshape(row_count, devices * out_columns)
        grad_keys, grad_values = dkv[0, 0], dkv[0, 1]
        grad_query = summed.reshape(row_count, columns)
    grad_hidden = lax.psum(hidden, "qry")
    return (grad_query, grad_keys, grad_values, grad_hidden)


def solution(mesh):
    in_specs = (
        P("psg", "qry"),
        P("psg", "qry"),
        P("psg", "qry"),
        P("qry", "psg"),
        P("psg", "qry"),
        P("psg", "qry"),
        P("psg", "qry"),
        P(),
        P(),
    )
    out_specs = (P("psg", "qry"), P("psg", "qry"), P("psg", "qry"), P("psg", None))
    return jax.shard_map(
        on_device, mesh=mesh, in_specs=in_specs, out_specs=out_specs, check_vma=False
    )
```
